128 devices in a mesh: grp: 4 (over y), patch: 32 (over z, x, core).
Axes of the slice: x: 4, y: 4, z: 4, core: 2. Of those that a mesh axis runs over, the one named last changes fastest.
Arguments:
- state: float32 [9, 60, 262144], P(None, 'grp', 'patch'), may hold values from -6 to 6
- courant_x: float32 [60, 262144], P('grp', 'patch'), may hold values from -0.45 to 0.45
- courant_y: float32 [60, 262144], P('grp', 'patch'), may hold values from -0.45 to 0.45
- surface: bfloat16 [16, 262144], P('grp', 'patch'), may hold values from -6 to 6
- w_in: bfloat16 [556, 256], replicated, may hold values from -0.25 to 0.25
- b_hidden: float32 [4, 256], replicated, may hold values from -3 to 3
- w_mid: bfloat16 [3, 256, 256], replicated, may hold values from -0.375 to 0.375
- w_out: bfloat16 [256, 540], replicated, may hold values from -0.375 to 0.375
- owner_map: int32 [2048, 1], replicated, may hold values from 0 to 31; in each aligned block of 16 rows (0 to 15, 16 to 31, ...) at most 2 rows name the same one
- neighbours: int32 [32, 4], replicated, may hold values from 0 to 31, as said below
Outputs:
- new_state: float32 [9, 60, 262144], P(None, 'grp', 'patch')
- owner_heating: float32 [256, 4096], P('grp', 'patch')
The draws below stay inside these ranges and needn't reach their ends.
Inputs may be any that keep to these rules, and one draw needn't show every extreme that they name: owner_map[b, 0] is the owner of block b (row b % 64 of patch b // 64); within each aligned run of 16 blocks no owner is named more than 2 times, and in some run one owner exactly 2 times. The patches tile a periodic arrangement of 4 by 8: neighbours[p, 0] and neighbours[p, 1] precede and follow p along the first direction, neighbours[p, 2] and neighbours[p, 3] along the second; neighbours[neighbours[p, 0], 1] = p, neighbours[neighbours[p, 2], 3] = p, and neighbours[neighbours[p, 0], 2] = neighbours[neighbours[p, 2], 0].
All inputs are finite; a program needn't handle non-finite values.
Results may differ from the reference program's by a relative error of at most 0.0059.
The reference program's roundings to bfloat16 on the way (of `features`, `hidden` and `tendency`) count: a program that leaves them out, or rounds other values in their place, can miss the bound.
Values may be sent and summed in bfloat16 or wider, within the bound.
A program may use at most 640 MiB of HBM per device.

```python
import math
import jax
import jax.numpy as jnp
import numpy as np
from jax import lax

VARS = 9
LEV = 60
SURF = 16
HID = 256
MIDS = 3
SUBSTEPS = 3
PY = 128
PX = 64
FEAT = 556
OUTF = 540
QB = 16
CAPQ = 2
COLS = 262144
BLOCKS = 2048
RSLOT = 256
PATCH_ROWS = 4
PATCH_COLS = 8
N_GRP = 4
N_PATCH = 32


def draw_state(key, part):
    value_key = jax.random.fold_in(key, 11)
    values = jax.random.normal(value_key, (VARS, LEV, COLS), jnp.float32)
    return jnp.clip(values, -6.0, 6.0).astype(jnp.float32)


def draw_neighbours(key, part):
    total = PATCH_ROWS * PATCH_COLS
    placed = jax.random.permutation(key, total).astype(jnp.int32)
    patch_at = jnp.argsort(placed, stable=True).astype(jnp.int32)
    row_pos = placed // PATCH_COLS
    col_pos = placed % PATCH_COLS
    north_id = patch_at[(row_pos - 1) % PATCH_ROWS * PATCH_COLS + col_pos]
    south_id = patch_at[(row_pos + 1) % PATCH_ROWS * PATCH_COLS + col_pos]
    west_id = patch_at[row_pos * PATCH_COLS + (col_pos - 1) % PATCH_COLS]
    east_id = patch_at[row_pos * PATCH_COLS + (col_pos + 1) % PATCH_COLS]
    return jnp.stack([north_id, south_id, west_id, east_id], axis=1).astype(jnp.int32)


def steps_of(rng, dims, shards, least, high):
    gain, own = 1.0, jax.random.fold_in(rng, 6)
    for position, blocks in shards:
        draws = jnp.exp(jax.random.uniform(jax.random.fold_in(own, position), (blocks,), jnp.float32, least / len(shards), high / len(shards)))
        gain = gain * jnp.repeat(draws, dims[position] // blocks).reshape([-1 if axis == position else 1 for axis in range(len(dims))])
    return gain


def deal_out(own_key, own, number, rows, number_of, top, reach, skew):
    order = jax.random.permutation(own_key, number_of)
    crowded, usual = portions_of(number_of, rows * top, reach, skew, True), portions_of(number_of, rows * top, reach, skew, False)
    places = jnp.arange(number_of)

    def named(tallies, turn):
        used = int((tallies > 0).sum())
        fixed = max(1, used // 4)
        shifted = fixed + (places - fixed + turn * (used - fixed)) % max(1, number_of - fixed)
        return jnp.zeros((number_of,), jnp.int32).at[order[jnp.where(places < fixed, places, shifted)]].set(jnp.asarray(tallies, jnp.int32))

    tallies = jnp.where(number % 4 == 0, named(crowded, number // 4), named(usual, number - number // 4 - 1))
    mixed = jax.random.permutation(jax.random.fold_in(own, 3), number_of)
    giver, sink = mixed[0:number_of // 2 * 2:2], mixed[1:number_of // 2 * 2:2]
    slack = jnp.minimum(tallies[giver] - 1, reach - tallies[sink]) // 2
    slack = jnp.where((giver == order[0]) | (sink == order[0]) | (tallies[sink] == 0), 0, jnp.maximum(slack, 0))
    shifted = jax.random.randint(jax.random.fold_in(own, 4), (number_of // 2,), 0, 1 << 20) % (slack + 1)
    tallies = tallies.at[giver].add(-shifted).at[sink].add(shifted)
    items = jnp.searchsorted(jnp.cumsum(tallies), jnp.arange(rows * top), side="right").astype(jnp.int32)
    grid = items.reshape(top, rows).T
    grid = grid[jax.random.permutation(jax.random.fold_in(own, 1), rows)]
    turn = jax.random.randint(jax.random.fold_in(own, 2), (rows, 1), 0, top)
    return jnp.take_along_axis(grid, (jnp.arange(top)[None, :] + turn) % top, axis=1)


def portions_of(count, total, limit, slope, full):
    weights = [(1 << 20) // math.isqrt(standing ** slope) + 1 for standing in range(1, count + 1)]
    largest = limit if full else min(limit, max(-(-total // count), total * weights[0] // sum(weights)))
    least = 1 if total - largest >= count - 1 else 0
    holding, spare = [largest] + [least] * (count - 1), total - largest - least * (count - 1)
    while spare > 0:
        movable = [i for i in range(1, count) if holding[i] < largest] or [i for i in range(1, count) if holding[i] < limit]
        whole, left = sum([weights[i] for i in movable]), spare
        for i in movable:
            more = min(limit - holding[i], max(1, left * weights[i] // whole), spare)
            holding[i] = holding[i] + more
            spare = spare - more
    return np.array(holding)


def centred(stream_key, shape, scale, limit, pieces=(), kind=jnp.bfloat16):
    factor_of = steps_of(stream_key, shape, pieces, -0.22, 0.18) if pieces else 1.0
    array = jax.random.normal(stream_key, shape, jnp.float32) * scale * factor_of
    return jnp.minimum(jnp.maximum(array, -limit), limit).astype(kind)


def setup_inputs(seed: int = 0) -> dict:
    key_of = jax.random.split(jax.random.key(seed), 11)
    state = draw_state(jax.random.fold_in(key_of[10], 71), 0)
    courant_x = jnp.clip(jax.random.uniform(key_of[1], (LEV, COLS), jnp.float32, -0.45, 0.45) * steps_of(key_of[1], (LEV, COLS), ((0, 4), (1, 32)), -0.4, 0.0), -0.45, 0.45)
    courant_y = jnp.clip(jax.random.uniform(key_of[2], (LEV, COLS), jnp.float32, -0.45, 0.45) * steps_of(key_of[2], (LEV, COLS), ((0, 4), (1, 32)), -0.4, 0.0), -0.45, 0.45)
    surface = centred(key_of[3], (SURF, COLS), 1.0, 6.0, ((0, 4), (1, 32)))
    w_in = centred(key_of[4], (FEAT, HID), FEAT ** -0.5, 0.25)
    b_hidden = centred(key_of[5], (MIDS + 1, HID), 0.5, 3.0, (), jnp.float32)
    w_mid = centred(key_of[6], (MIDS, HID, HID), HID ** -0.5, 0.375)
    w_out = centred(key_of[7], (HID, OUTF), HID ** -0.5, 0.375)
    owner_map_keys = jax.random.split(jax.random.fold_in(key_of[8], 1), BLOCKS // QB)
    owner_map_turns = jax.random.permutation(jax.random.fold_in(key_of[8], 3), BLOCKS // QB)
    owner_map = jax.vmap(lambda own, number: deal_out(jax.random.fold_in(key_of[8], 2), own, number, QB, N_PATCH, 1, CAPQ, 2))(owner_map_keys, owner_map_turns).reshape((BLOCKS, 1))
    neighbours = draw_neighbours(jax.random.fold_in(key_of[10], 71), 0)
    return dict(state=state, courant_x=courant_x, courant_y=courant_y, surface=surface, w_in=w_in, b_hidden=b_hidden, w_mid=w_mid, w_out=w_out, owner_map=owner_map, neighbours=neighbours)


KAPPA = 0.24
PHYS_DT = 0.05
HEAT_WEIGHT = 0.125


def advance_grid(tracer, along_x, along_y, neighbours):
    northern = jnp.concatenate([tracer[:, neighbours[:, 0], -1:, :], tracer[:, :, :-1, :]], axis=2)
    southern = jnp.concatenate([tracer[:, :, 1:, :], tracer[:, neighbours[:, 1], :1, :]], axis=2)
    western = jnp.concatenate([tracer[:, neighbours[:, 2], :, -1:], tracer[:, :, :, :-1]], axis=3)
    eastern = jnp.concatenate([tracer[:, :, :, 1:], tracer[:, neighbours[:, 3], :, :1]], axis=3)
    return tracer - 0.5 * along_x * (southern - northern) - 0.5 * along_y * (eastern - western) + KAPPA * (northern + southern + western + eastern - 4.0 * tracer)


def activate(pre_act):
    return lax.optimization_barrier(jax.nn.silu(pre_act).astype(jnp.bfloat16)).astype(jnp.float32)


def reference(state, courant_x, courant_y, surface, w_in, b_hidden, w_mid, w_out, owner_map, neighbours):
    grid_x = courant_x.reshape(LEV, N_PATCH, PX, PY)
    grid_y = courant_y.reshape(LEV, N_PATCH, PX, PY)

    def dynamics(tracer):
        tracer = tracer.reshape(LEV, N_PATCH, PX, PY)
        for substep_index in range(SUBSTEPS):
            tracer = advance_grid(tracer, grid_x, grid_y, neighbours)
        return tracer.reshape(LEV, COLS)

    advected = lax.map(dynamics, state)
    weights_in = w_in.astype(jnp.float32)
    weights_mid = w_mid.astype(jnp.float32)
    weights_out = w_out.astype(jnp.float32)
    highest = lax.Precision.HIGHEST

    def physics(patch_index):
        start = patch_index * PX * PY
        columns = lax.dynamic_slice_in_dim(state, start, PX * PY, 2).reshape(VARS * LEV, PX * PY)
        surf_cols = lax.dynamic_slice_in_dim(surface, start, PX * PY, 1).astype(jnp.float32)
        features = jnp.concatenate([columns, surf_cols], axis=0).astype(jnp.bfloat16)
        features = lax.optimization_barrier(features).astype(jnp.float32)
        hidden = activate(jnp.dot(features.T, weights_in, precision=highest) + b_hidden[0])
        for layer_index in range(MIDS):
            hidden = activate(jnp.dot(hidden, weights_mid[layer_index], precision=highest) + b_hidden[layer_index + 1])
        tendency = jnp.dot(hidden, weights_out, precision=highest).astype(jnp.bfloat16)
        return tendency.T

    tendencies = lax.map(physics, jnp.arange(N_PATCH, dtype=jnp.int32))
    tendency_grid = tendencies.reshape(N_PATCH, VARS, LEV, PX * PY).transpose(1, 2, 0, 3).reshape(VARS, LEV, COLS)
    new_state = advected + PHYS_DT * tendency_grid.astype(jnp.float32)
    heating = HEAT_WEIGHT * jnp.sum(tendencies[:, :LEV].astype(jnp.float32), axis=1)
    heating = heating.reshape(N_PATCH, N_GRP, QB, PY)
    owners = owner_map.reshape(N_PATCH, N_GRP, QB).astype(jnp.int32)
    matches = (owners[..., None] == jnp.arange(N_PATCH, dtype=jnp.int32)).astype(jnp.int32)
    before = jnp.cumsum(matches, axis=2) - matches
    slot_rank = jnp.sum(before * matches, axis=3).astype(jnp.int32)
    patch_ids = jnp.arange(N_PATCH, dtype=jnp.int32)[:, None, None]
    group_ids = jnp.arange(N_GRP, dtype=jnp.int32)[None, :, None]
    slot_rows = ((group_ids * N_PATCH + patch_ids) * CAPQ + slot_rank).astype(jnp.int32)
    slot_table = jnp.zeros((RSLOT, N_PATCH, PY), jnp.float32).at[slot_rows, owners].set(heating)
    return new_state, slot_table.reshape(RSLOT, N_PATCH * PY)
```

```python
import jax
import jax.numpy as jnp
from jax import lax
from jax.experimental import pallas as pl
from jax.experimental.pallas import tpu as pltpu
from jax.sharding import PartitionSpec as P

MESH = pl.DeviceIdType.MESH
F32 = jnp.float32
BF16 = jnp.bfloat16

VARS = 9
LEV = 60
SHARE = 15
SURF = 16
SSHARE = 4
HID = 256
MIDS = 3
PX = 64
LANES = 128
COLS = PX * LANES
QUARTER = COLS // 4
ROWS = VARS * 16
FEAT = 556
OUTF = 540
CHUNKS = 4
WIDE = QUARTER // CHUNKS
HALF = WIDE // 2
ROUNDS = 3
SPLIT = 5
GROUP_VARS = ((0, SPLIT), (SPLIT, VARS))
GROUP_ROWS = (SPLIT * 16, (VARS - SPLIT) * 16)

KAPPA = 0.24
PHYS_DT = 0.05
HEAT_WEIGHT = 0.125


def kernel(
    owner_ref, nbr_ref, state, courx, coury, surf, w_in, b_hid, w_mid, w_out,
    out, heat_out,
    S, T1, T2, CX, CY, F, X, FP, FM, TO, TR, OP, OM,
    W1, WM, W2, BB, CB, HT, PK, PR,
    GA0, GB0, SA0, SB0, RA0, RB0, GA1, GB1, SA1, SB1, RA1, RB1, GA2, GB2, SA2, SB2, RA2, RB2,
    load_sem, cour_sem, store_sem,
    in_s, in_r, fw_s, fw_r, out_s, out_r, of_s, of_r,
    p1_s, p1_r, p2_s, p2_r, p3_s, p3_r, ht_s, ht_r,
):
    g = lax.axis_index("grp")
    p = lax.axis_index("patch")
    zi, xi, ci = p // 8, (p // 2) % 4, p % 2
    gp, gm, go = (g + 1) % 4, (g + 3) % 4, (g + 2) % 4

    def rcopy(src, dst, ss, rs, dev):
        return pltpu.make_async_remote_copy(
            src_ref=src, dst_ref=dst, send_sem=ss, recv_sem=rs, device_id=dev, device_id_type=MESH
        )

    def col0(q, c):
        return pl.multiple_of(q * QUARTER + c * WIDE, LANES)

    order = (go, gp, gm, g)

    def load(c, i):
        off = col0(order[i], c)
        return pltpu.make_async_copy(
            state.at[:, :, pl.ds(off, WIDE)],
            S.at[:, :, pl.ds(pl.multiple_of(off + LANES, LANES), WIDE)],
            load_sem.at[c, i],
        )

    for c in range(CHUNKS):
        for i in range(4):
            load(c, i).start()
    cour = (
        pltpu.make_async_copy(courx, CX, cour_sem.at[0]),
        pltpu.make_async_copy(coury, CY, cour_sem.at[1]),
    )
    for copy in cour:
        copy.start()

    barrier = pltpu.get_barrier_semaphore()
    for other in (gp, gm, go):
        pl.semaphore_signal(barrier, inc=1, device_id=(other, p), device_id_type=MESH)

    def greet(d, carry):
        pl.semaphore_signal(barrier, inc=1, device_id=(g, (p + d) % 32), device_id_type=MESH)
        return carry

    lax.fori_loop(1, 32, greet, 0)
    pl.semaphore_wait(barrier, 34)

    def cast(q, c, own):
        off = col0(q, c)
        here = pl.multiple_of(off + LANES, LANES)
        for v in range(VARS):
            value = S[v, :, pl.ds(here, WIDE)]
            if v < SSHARE:
                extra = surf[v : v + 1, pl.ds(off, WIDE)].astype(F32)
            else:
                extra = jnp.zeros((1, WIDE), F32)
            value = jnp.concatenate([value, extra], axis=0).astype(BF16)
            F[q, pl.ds(v * 16, 16), pl.ds(c * WIDE, WIDE)] = value
            if own:
                X[pl.ds(pl.multiple_of(g * ROWS + v * 16, 16), 16), pl.ds(c * WIDE, WIDE)] = value

    mine = pl.ds(pl.multiple_of(g * ROWS, 16), ROWS)
    prev_rows = pl.ds(pl.multiple_of(gm * ROWS, 16), ROWS)
    next_rows = pl.ds(pl.multiple_of(gp * ROWS, 16), ROWS)
    far_rows = pl.ds(pl.multiple_of(go * ROWS, 16), ROWS)

    def in_copies(c):
        lo, hi, whole = pl.ds(c * WIDE, HALF), pl.ds(c * WIDE + HALF, HALF), pl.ds(c * WIDE, WIDE)
        return (
            rcopy(F.at[go, :, lo], FP.at[c], in_s.at[c, 0], in_r.at[c, 0], (gp, p)),
            rcopy(F.at[go, :, hi], FM.at[c], in_s.at[c, 1], in_r.at[c, 1], (gm, p)),
            rcopy(F.at[gp, :, whole], X.at[mine, whole], in_s.at[c, 2], in_r.at[c, 2], (gp, p)),
            rcopy(F.at[gm, :, whole], X.at[mine, whole], in_s.at[c, 3], in_r.at[c, 3], (gm, p)),
        )

    def in_forwards(c):
        lo, hi = pl.ds(c * WIDE, HALF), pl.ds(c * WIDE + HALF, HALF)
        return (
            rcopy(FP.at[c], X.at[prev_rows, lo], fw_s.at[c, 0], fw_r.at[c, 0], (gp, p)),
            rcopy(FM.at[c], X.at[next_rows, hi], fw_s.at[c, 1], fw_r.at[c, 1], (gm, p)),
        )

    def out_copies(c):
        lo, hi, whole = pl.ds(c * WIDE, HALF), pl.ds(c * WIDE + HALF, HALF), pl.ds(c * WIDE, WIDE)
        return (
            rcopy(TO.at[far_rows, lo], OP.at[c], out_s.at[c, 0], out_r.at[c, 0], (gp, p)),
            rcopy(TO.at[far_rows, hi], OM.at[c], out_s.at[c, 1], out_r.at[c, 1], (gm, p)),
            rcopy(TO.at[next_rows, whole], TR.at[g, :, whole], out_s.at[c, 2], out_r.at[c, 2], (gp, p)),
            rcopy(TO.at[prev_rows, whole], TR.at[g, :, whole], out_s.at[c, 3], out_r.at[c, 3], (gm, p)),
        )

    def out_forwards(c):
        lo, hi = pl.ds(c * WIDE, HALF), pl.ds(c * WIDE + HALF, HALF)
        return (
            rcopy(OP.at[c], TR.at[gm, :, lo], of_s.at[c, 0], of_r.at[c, 0], (gp, p)),
            rcopy(OM.at[c], TR.at[gp, :, hi], of_s.at[c, 1], of_r.at[c, 1], (gm, p)),
        )

    for c in range(CHUNKS):
        for i in range(3):
            load(c, i).wait()
            cast(order[i], c, False)
            copies = in_copies(c)
            if i == 0:
                copies[0].start()
                copies[1].start()
            else:
                copies[i + 1].start()
    for c in range(CHUNKS):
        load(c, 3).wait()
        cast(g, c, True)

    halo = (
        ((GA0, SA0, RA0), (GB0, SB0, RB0)),
        ((GA1, SA1, RA1), (GB1, SB1, RB1)),
        ((GA2, SA2, RA2), (GB2, SB2, RB2)),
    )
    first = (xi, zi)
    second = (zi, xi)
    even = lax.broadcasted_iota(jnp.int32, (16, LANES), 1) % 2 == 0

    def patch_of(k, one, two, core):
        return two * 8 + one * 2 + core if k == 0 else one * 8 + two * 2 + core

    def spots(k, n):
        z, x, core = n // 8, (n // 2) % 4, n % 2
        return (x, z, core) if k == 0 else (z, x, core)

    def p1_copies(r, k):
        G = halo[r][k][0]
        return [
            rcopy(
                G.at[ci, first[k]], G.at[ci, first[k]], p1_s.at[r, k, d - 1], p1_r.at[r, k, d - 1],
                (g, patch_of(k, (first[k] + d) % 4, second[k], ci)),
            )
            for d in (2, 1, 3)
        ]

    def p2_copy(r, k):
        G = halo[r][k][0]
        return rcopy(
            G.at[ci], G.at[ci], p2_s.at[r, k], p2_r.at[r, k],
            (g, patch_of(k, first[k], second[k], 1 - ci)),
        )

    def p3_copy(r, k, d):
        _, Sd, R = halo[r][k]
        return rcopy(
            Sd.at[d], R.at[second[k]], p3_s.at[r, k, d - 1], p3_r.at[r, k, d - 1],
            (g, patch_of(k, first[k], (second[k] + d) % 4, ci)),
        )

    def put_edge(r, strip, v, value):
        k = 0 if v < SPLIT else 1
        G = halo[r][k][0]
        G[ci, first[k], strip, pl.ds((v - GROUP_VARS[k][0]) * 16, 16), :] = jnp.concatenate(
            [value, jnp.zeros((1, LANES), F32)], axis=0
        ).astype(BF16)

    def start_p1(r):
        for k in range(2):
            for copy in p1_copies(r, k):
                copy.start()

    def start_p2(r):
        for k in range(2):
            for copy in p1_copies(r, k):
                copy.wait_recv()
            p2_copy(r, k).start()

    def start_p3(r):
        for k in range(2):
            G, Sd, R = halo[r][k]
            p2_copy(r, k).wait_recv()
            for d in (2, 1, 3, 0):
                t = patch_of(k, first[k], (second[k] + d) % 4, ci)
                at = [spots(k, nbr_ref[j, t]) for j in range(4)]
                north = G[at[0][2], at[0][0], 1]
                south = G[at[1][2], at[1][0], 0]
                if d == 0:
                    R[second[k], 0] = north
                    R[second[k], 1] = south
                else:
                    Sd[d, 0] = north
                    Sd[d, 1] = south
                for v in range(GROUP_ROWS[k] // 16):
                    rows = pl.ds(v * 16, 16)
                    west = G[at[2][2], at[2][0], 2, rows].astype(F32)
                    east = G[at[3][2], at[3][0], 2, rows].astype(F32)
                    mixed = jnp.where(even, east, west).astype(BF16)
                    if d == 0:
                        R[second[k], 2, rows] = mixed
                    else:
                        Sd[d, 2, rows] = mixed
                if d:
                    p3_copy(r, k, d).start()

    def finish_halo(r, T):
        for k in range(2):
            R = halo[r][k][2]
            for d in (2, 1, 3):
                p3_copy(r, k, d).wait_recv()
            at = [spots(k, nbr_ref[j, p])[1] for j in range(4)]
            for v in range(*GROUP_VARS[k]):
                rows = pl.ds((v - GROUP_VARS[k][0]) * 16, 16)
                T[v, :, pl.ds(0, LANES)] = R[at[0], 0, rows].astype(F32)[:SHARE]
                T[v, :, pl.ds(LANES + COLS, LANES)] = R[at[1], 1, rows].astype(F32)[:SHARE]
                west = pltpu.roll(R[at[2], 2, rows].astype(F32), 1, 1)
                east = pltpu.roll(R[at[3], 2, rows].astype(F32), LANES - 1, 1)
                CB[v] = jnp.where(even, west, east)[:SHARE]

    lane = lax.broadcasted_iota(jnp.int32, (SHARE, LANES), 1)

    def strip_mask(x):
        return (lane == 2 * x) | (lane == (2 * x + LANES - 1) % LANES)

    def first_edges():
        def step(x, acc):
            mask = strip_mask(x)
            here = pl.ds(pl.multiple_of((x + 1) * LANES, LANES), LANES)
            return tuple(
                jnp.where(mask, pltpu.roll(S[v, :, here], 2 * x, 1), acc[v]) for v in range(VARS)
            )

        zero = jnp.zeros((SHARE, LANES), F32)
        acc = lax.fori_loop(0, PX, step, (zero,) * VARS)
        for v in range(VARS):
            put_edge(0, 0, v, S[v, :, pl.ds(LANES, LANES)])
            put_edge(0, 1, v, S[v, :, pl.ds(COLS, LANES)])
            put_edge(0, 2, v, acc[v])

    def substep(T, N, r):
        def step(x, acc):
            here = pl.ds(pl.multiple_of((x + 1) * LANES, LANES), LANES)
            above = pl.ds(pl.multiple_of(x * LANES, LANES), LANES)
            below = pl.ds(pl.multiple_of((x + 2) * LANES, LANES), LANES)
            flat = pl.ds(pl.multiple_of(x * LANES, LANES), LANES)
            hx = 0.5 * CX[:, flat]
            hy = 0.5 * CY[:, flat]
            cn, cs, cw, ce = KAPPA + hx, KAPPA - hx, KAPPA + hy, KAPPA - hy
            mask = strip_mask(x)
            new_acc = []
            for v in range(VARS):
                c = T[v, :, here]
                edge = pltpu.roll(CB[v], (LANES - 2 * x) % LANES, 1)
                w = jnp.where(lane == 0, edge, pltpu.roll(c, 1, 1))
                e = jnp.where(lane == LANES - 1, edge, pltpu.roll(c, LANES - 1, 1))
                new = (
                    (1.0 - 4.0 * KAPPA) * c
                    + (cn * T[v, :, above] + cs * T[v, :, below])
                    + (cw * w + ce * e)
                )
                N[v, :, here] = new
                if r is not None:
                    new_acc.append(jnp.where(mask, pltpu.roll(new, 2 * x, 1), acc[v]))
            return tuple(new_acc)

        zero = jnp.zeros((SHARE, LANES), F32)
        acc = lax.fori_loop(0, PX, step, (zero,) * VARS if r is not None else ())
        if r is not None:
            for v in range(VARS):
                put_edge(r, 0, v, N[v, :, pl.ds(LANES, LANES)])
                put_edge(r, 1, v, N[v, :, pl.ds(COLS, LANES)])
                put_edge(r, 2, v, acc[v])

    def prepare():
        j = lax.broadcasted_iota(jnp.int32, (4 * ROWS, 1), 0)
        grp = (j >= ROWS).astype(jnp.int32) + (j >= 2 * ROWS).astype(jnp.int32) + (j >= 3 * ROWS).astype(jnp.int32)
        rest = j - grp * ROWS
        var, lev = rest >> 4, rest & 15
        state_row = var * LEV + grp * SHARE + lev
        surf_row = jnp.where(var < SSHARE, VARS * LEV + grp * SSHARE + var, -1)
        source = jnp.where(lev < SHARE, state_row, surf_row)
        pick = (source == lax.broadcasted_iota(jnp.int32, (4 * ROWS, FEAT), 1)).astype(F32).astype(BF16)
        placed = jnp.dot(pick, w_in[...], preferred_element_type=F32)
        W1[...] = placed.T.astype(BF16)
        source = jnp.where(lev < SHARE, state_row, -1)
        pick = (source == lax.broadcasted_iota(jnp.int32, (4 * ROWS, OUTF), 1)).astype(F32).astype(BF16)
        W2[...] = jnp.dot(pick, w_out[...], preferred_element_type=F32).astype(BF16)
        for i in range(MIDS):
            WM[i] = w_mid[i].astype(F32).T.astype(BF16)
        for i in range(MIDS + 1):
            BB[i] = jnp.broadcast_to(b_hid[i : i + 1, :], (LANES, HID)).T

    def silu(i, pre):
        half = 0.5 * (pre + jnp.concatenate([BB[i]] * (WIDE // LANES), axis=1))
        return (half + half * jnp.tanh(half)).astype(BF16)

    def physics(c):
        whole = pl.ds(c * WIDE, WIDE)
        in_copies(c)[2].wait_recv()
        in_copies(c)[3].wait_recv()
        for copy in in_forwards(c):
            copy.wait_recv()
        hidden = silu(0, jnp.dot(W1[...], X[:, whole], preferred_element_type=F32))
        for i in range(MIDS):
            hidden = silu(i + 1, jnp.dot(WM[i], hidden, preferred_element_type=F32))
        total = jnp.zeros((1, WIDE), F32)
        level = lax.broadcasted_iota(jnp.int32, (16, WIDE), 0)
        for d in range(4):
            tend = jnp.dot(W2[pl.ds(d * ROWS, ROWS)], hidden, preferred_element_type=F32).astype(BF16)
            TO[pl.ds(d * ROWS, ROWS), whole] = tend
            first_var = jnp.where(level < SHARE, tend[:16].astype(F32), 0.0)
            total = total + jnp.sum(first_var, axis=0, keepdims=True)
        total = HEAT_WEIGHT * total
        for i in range(WIDE // LANES):
            HT[pl.ds(c * (WIDE // LANES) + i, 1), :] = total[:, i * LANES : (i + 1) * LANES]
        for copy in out_copies(c):
            copy.start()

    def forward_in(c):
        copies = in_copies(c)
        forwards = in_forwards(c)
        for i in range(2):
            copies[i].wait_recv()
            forwards[i].start()

    def forward_out(c):
        copies = out_copies(c)
        forwards = out_forwards(c)
        for i in range(2):
            copies[i].wait_recv()
            forwards[i].start()

    def heat_copy(d):
        o = (p + d) % 32
        return rcopy(
            PK.at[o], PR.at[p], ht_s.at[d - 1], ht_r.at[d - 1], (g, o)
        )

    def send_heating():
        owner = [owner_ref[p * PX + g * 16 + b] for b in range(16)]
        slot = []
        for b in range(16):
            rank = jnp.int32(0)
            for before in range(b):
                rank = rank + (owner[before] == owner[b]).astype(jnp.int32)
            slot.append(owner[b] * 2 + rank)
        sub = lax.broadcasted_iota(jnp.int32, (8, LANES), 0)
        lines = [jnp.broadcast_to(HT[pl.ds(b, 1), :], (8, LANES)) for b in range(16)]

        def fill(o, carry):
            rows = sub + o * 2
            block = jnp.zeros((8, LANES), F32)
            for b in range(16):
                block = jnp.where(rows == slot[b], lines[b], block)
            PK[o] = block
            return carry

        lax.fori_loop(0, 32, fill, 0)
        PR[p] = PK[p]

        def send(d, carry):
            heat_copy(d).start()
            return carry

        lax.fori_loop(1, 32, send, 0)

    def finish_heating():
        def wait(d, carry):
            heat_copy(d).wait()
            return carry

        lax.fori_loop(1, 32, wait, 0)
        for o in range(32):
            heat_out[pl.ds(o * 2, 2), :] = PR[o, pl.ds(0, 2), :]

    def store(q, c, i):
        off = col0(q, c)
        return pltpu.make_async_copy(
            T1.at[:, :, pl.ds(pl.multiple_of(off + LANES, LANES), WIDE)],
            out.at[:, :, pl.ds(off, WIDE)],
            store_sem.at[c, i],
        )

    def finish(c):
        for copy in out_forwards(c):
            copy.wait_recv()
        out_copies(c)[2].wait_recv()
        out_copies(c)[3].wait_recv()
        whole = pl.ds(c * WIDE, WIDE)
        for i, q in enumerate(order):
            here = pl.ds(pl.multiple_of(col0(q, c) + LANES, LANES), WIDE)
            for v in range(VARS):
                rows = pl.ds(v * 16, 16)
                if i == 3:
                    tend = TO[pl.ds(pl.multiple_of(g * ROWS + v * 16, 16), 16), whole]
                else:
                    tend = TR[q, rows, whole]
                T1[v, :, here] = T1[v, :, here] + PHYS_DT * tend.astype(F32)[:SHARE]
            store(q, c, i).start()

    first_edges()
    start_p1(0)
    prepare()
    forward_in(0)
    start_p2(0)
    for copy in cour:
        copy.wait()
    start_p3(0)
    forward_in(1)
    physics(0)
    finish_halo(0, S)
    substep(S, T1, 1)
    start_p1(1)
    forward_in(2)
    physics(1)
    forward_in(3)
    start_p2(1)
    forward_out(0)
    start_p3(1)
    physics(2)
    finish_halo(1, T1)
    substep(T1, T2, 2)
    start_p1(2)
    forward_out(1)
    physics(3)
    send_heating()
    start_p2(2)
    forward_out(2)
    start_p3(2)
    forward_out(3)
    finish_halo(2, T2)
    substep(T2, T1, None)
    for c in range(CHUNKS):
        finish(c)
    finish_heating()
    for c in range(CHUNKS):
        for copy in in_copies(c) + in_forwards(c) + out_copies(c) + out_forwards(c):
            copy.wait_send()
        for i in range(4):
            store(order[i], c, i).wait()
    for r in range(ROUNDS):
        for k in range(2):
            for copy in p1_copies(r, k):
                copy.wait_send()
            p2_copy(r, k).wait_send()
            for d in (1, 2, 3):
                p3_copy(r, k, d).wait_send()


def on_device(
    state, courant_x, courant_y, surface, w_in, b_hidden, w_mid, w_out, owner_map, neighbours
):
    smem = pl.BlockSpec(memory_space=pltpu.SMEM)
    vmem = pl.BlockSpec(memory_space=pltpu.VMEM)
    anyw = pl.BlockSpec(memory_space=pl.ANY)
    dma = pltpu.SemaphoreType.DMA
    padded = pltpu.VMEM((VARS, SHARE, COLS + 2 * LANES), F32)
    halo_shapes = []
    for lead in ((2, 4, 3), (4, 3), (4, 3)) * ROUNDS:
        for rows in GROUP_ROWS:
            halo_shapes.append(pltpu.VMEM(lead + (rows, LANES), BF16))
    return pl.pallas_call(
        kernel,
        name="couple",
        out_shape=(
            jax.ShapeDtypeStruct((VARS, SHARE, COLS), F32),
            jax.ShapeDtypeStruct((64, LANES), F32),
        ),
        in_specs=[smem, smem, anyw, anyw, anyw] + [vmem] * 5,
        out_specs=(anyw, vmem),
        scratch_shapes=[
            padded, padded, padded,
            pltpu.VMEM((SHARE, COLS), F32), pltpu.VMEM((SHARE, COLS), F32),
            pltpu.VMEM((4, ROWS, QUARTER), BF16),
            pltpu.VMEM((4 * ROWS, QUARTER), BF16),
            pltpu.VMEM((CHUNKS, ROWS, HALF), BF16), pltpu.VMEM((CHUNKS, ROWS, HALF), BF16),
            pltpu.VMEM((4 * ROWS, QUARTER), BF16),
            pltpu.VMEM((4, ROWS, QUARTER), BF16),
            pltpu.VMEM((CHUNKS, ROWS, HALF), BF16), pltpu.VMEM((CHUNKS, ROWS, HALF), BF16),
            pltpu.VMEM((HID, 4 * ROWS), BF16),
            pltpu.VMEM((MIDS, HID, HID), BF16),
            pltpu.VMEM((4 * ROWS, HID), BF16),
            pltpu.VMEM((MIDS + 1, HID, LANES), F32),
            pltpu.VMEM((VARS, SHARE, LANES), F32),
            pltpu.VMEM((16, LANES), F32),
            pltpu.VMEM((32, 8, LANES), F32),
            pltpu.VMEM((32, 8, LANES), F32),
            *halo_shapes,
            dma((CHUNKS, 4)), dma((2,)), dma((CHUNKS, 4)),
            dma((CHUNKS, 4)), dma((CHUNKS, 4)), dma((CHUNKS, 2)), dma((CHUNKS, 2)),
            dma((CHUNKS, 4)), dma((CHUNKS, 4)), dma((CHUNKS, 2)), dma((CHUNKS, 2)),
            dma((ROUNDS, 2, 3)), dma((ROUNDS, 2, 3)), dma((ROUNDS, 2)), dma((ROUNDS, 2)),
            dma((ROUNDS, 2, 3)), dma((ROUNDS, 2, 3)), dma((31,)), dma((31,)),
        ],
        compiler_params=pltpu.CompilerParams(
            collective_id=0, has_side_effects=True, vmem_limit_bytes=56 * 2**20
        ),
    )(
        owner_map.reshape(-1), neighbours.T, state, courant_x, courant_y, surface,
        w_in, b_hidden, w_mid, w_out.T,
    )


def solution(mesh):
    placed = (
        P(None, "grp", "patch"), P("grp", "patch"), P("grp", "patch"), P("grp", "patch"),
        P(), P(), P(), P(), P(), P(),
    )
    return jax.shard_map(
        on_device,
        mesh=mesh,
        in_specs=placed,
        out_specs=(P(None, "grp", "patch"), P("grp", "patch")),
        check_vma=False,
    )
```

```python
import jax
import jax.numpy as jnp
from jax import lax
from jax.experimental import pallas as pl
from jax.experimental.pallas import tpu as pltpu
from jax.sharding import PartitionSpec as P

MESH = pl.DeviceIdType.MESH
F32 = jnp.float32
BF16 = jnp.bfloat16

VARS = 9
LEV = 60
SHARE = 15
SURF = 16
SSHARE = 4
HID = 256
MIDS = 3
PX = 64
LANES = 128
COLS = PX * LANES
QUARTER = COLS // 4
ROWS = VARS * 16
FEAT = 556
OUTF = 540
CHUNKS = 4
WIDE = QUARTER // CHUNKS
HALF = WIDE // 2
ROUNDS = 3
SPLIT = 5
GROUP_VARS = ((0, SPLIT), (SPLIT, VARS))
GROUP_ROWS = (SPLIT * 16, (VARS - SPLIT) * 16)

KAPPA = 0.24
PHYS_DT = 0.05
HEAT_WEIGHT = 0.125


def kernel(
    owner_ref, nbr_ref, state, courx, coury, surf_in, w_in_in, b_hid_in, w_mid_in, w_out_in,
    out, heat_out,
    ST, S, T1, CX, CY, HX, HY, surf, w_in, b_hid, w_mid, w_out,
    F, X, FP, FM, TO, TR, OP, OM,
    W1, WM, W2, BB, CB, EX, HT, PK, HZ, HZ2, HXX, HC, HR,
    GA0, GB0, SA0, SB0, RA0, RB0, GA1, GB1, SA1, SB1, RA1, RB1, GA2, GB2, SA2, SB2, RA2, RB2,
    load_sem, cour_sem, par_sem,
    in_s, in_r, fw_s, fw_r, out_s, out_r, of_s, of_r,
    p1_s, p1_r, p2_s, p2_r, p3_s, p3_r, hz_s, hz_r, hx_s, hx_r, hc_s, hc_r,
):
    g = lax.axis_index("grp")
    p = lax.axis_index("patch")
    zi, xi, ci = p // 8, (p // 2) % 4, p % 2
    gp, gm, go = (g + 1) % 4, (g + 3) % 4, (g + 2) % 4

    def rcopy(src, dst, ss, rs, dev):
        return pltpu.make_async_remote_copy(
            src_ref=src, dst_ref=dst, send_sem=ss, recv_sem=rs, device_id=dev, device_id_type=MESH
        )

    def col0(q, c):
        return pl.multiple_of(q * QUARTER + c * WIDE, LANES)

    order = (go, gp, gm, g)

    def load(c, i):
        off = col0(order[i], c)
        return pltpu.make_async_copy(
            state.at[:, :, pl.ds(off, WIDE)],
            ST.at[:, :, pl.ds(off, WIDE)],
            load_sem.at[c, i],
        )

    params = tuple(
        pltpu.make_async_copy(src, dst, par_sem.at[i])
        for i, (src, dst) in enumerate(
            ((surf_in, surf), (w_in_in, w_in), (b_hid_in, b_hid), (w_mid_in, w_mid), (w_out_in, w_out))
        )
    )
    cour = (
        pltpu.make_async_copy(courx, CX, cour_sem.at[0]),
        pltpu.make_async_copy(coury, CY, cour_sem.at[1]),
    )

    barrier = pltpu.get_barrier_semaphore()
    for other in (gp, gm, go):
        pl.semaphore_signal(barrier, inc=1, device_id=(other, p), device_id_type=MESH)
    for d in (1, 2, 3):
        pl.semaphore_signal(
            barrier, inc=1, device_id=(g, zi * 8 + ((xi + d) % 4) * 2 + ci), device_id_type=MESH
        )
        pl.semaphore_signal(
            barrier, inc=1, device_id=(g, ((zi + d) % 4) * 8 + xi * 2 + ci), device_id_type=MESH
        )
    pl.semaphore_signal(barrier, inc=1, device_id=(g, p + 1 - 2 * ci), device_id_type=MESH)

    params[0].start()
    for c in range(CHUNKS):
        for i in range(4):
            load(c, i).start()
    for copy in params[1:] + cour:
        copy.start()
    params[0].wait()
    pl.semaphore_wait(barrier, 10)

    def cast(q, c, own):
        off = col0(q, c)
        here = pl.multiple_of(off + LANES, LANES)
        for v in range(VARS):
            value = ST[v, :, pl.ds(off, WIDE)]
            if v < SSHARE:
                extra = surf[v : v + 1, pl.ds(off, WIDE)].astype(F32)
            else:
                extra = jnp.zeros((1, WIDE), F32)
            value = jnp.concatenate([value, extra], axis=0)
            S[v, :, pl.ds(here, WIDE)] = value
            value = value.astype(BF16)
            if not own:
                F[q, pl.ds(v * 16, 16), pl.ds(c * WIDE, WIDE)] = value
            else:
                X[pl.ds(pl.multiple_of(g * ROWS + v * 16, 16), 16), pl.ds(c * WIDE, WIDE)] = value

    mine = pl.ds(pl.multiple_of(g * ROWS, 16), ROWS)
    prev_rows = pl.ds(pl.multiple_of(gm * ROWS, 16), ROWS)
    next_rows = pl.ds(pl.multiple_of(gp * ROWS, 16), ROWS)
    far_rows = pl.ds(pl.multiple_of(go * ROWS, 16), ROWS)

    def in_copies(c):
        lo, hi, whole = pl.ds(c * WIDE, HALF), pl.ds(c * WIDE + HALF, HALF), pl.ds(c * WIDE, WIDE)
        return (
            rcopy(F.at[go, :, lo], FP.at[c], in_s.at[c, 0], in_r.at[c, 0], (gp, p)),
            rcopy(F.at[go, :, hi], FM.at[c], in_s.at[c, 1], in_r.at[c, 1], (gm, p)),
            rcopy(F.at[gp, :, whole], X.at[mine, whole], in_s.at[c, 2], in_r.at[c, 2], (gp, p)),
            rcopy(F.at[gm, :, whole], X.at[mine, whole], in_s.at[c, 3], in_r.at[c, 3], (gm, p)),
        )

    def in_forwards(c):
        lo, hi = pl.ds(c * WIDE, HALF), pl.ds(c * WIDE + HALF, HALF)
        return (
            rcopy(FP.at[c], X.at[prev_rows, lo], fw_s.at[c, 0], fw_r.at[c, 0], (gp, p)),
            rcopy(FM.at[c], X.at[next_rows, hi], fw_s.at[c, 1], fw_r.at[c, 1], (gm, p)),
        )

    def out_copies(c):
        lo, hi, whole = pl.ds(c * WIDE, HALF), pl.ds(c * WIDE + HALF, HALF), pl.ds(c * WIDE, WIDE)
        return (
            rcopy(TO.at[far_rows, lo], OP.at[c], out_s.at[c, 0], out_r.at[c, 0], (gp, p)),
            rcopy(TO.at[far_rows, hi], OM.at[c], out_s.at[c, 1], out_r.at[c, 1], (gm, p)),
            rcopy(TO.at[next_rows, whole], TR.at[g, :, whole], out_s.at[c, 2], out_r.at[c, 2], (gp, p)),
            rcopy(TO.at[prev_rows, whole], TR.at[g, :, whole], out_s.at[c, 3], out_r.at[c, 3], (gm, p)),
        )

    def out_forwards(c):
        lo, hi = pl.ds(c * WIDE, HALF), pl.ds(c * WIDE + HALF, HALF)
        return (
            rcopy(OP.at[c], TR.at[gm, :, lo], of_s.at[c, 0], of_r.at[c, 0], (gp, p)),
            rcopy(OM.at[c], TR.at[gp, :, hi], of_s.at[c, 1], of_r.at[c, 1], (gm, p)),
        )

    for c in range(CHUNKS):
        for i in range(3):
            load(c, i).wait()
            cast(order[i], c, False)
            copies = in_copies(c)
            if i == 0:
                copies[0].start()
                copies[1].start()
            else:
                copies[i + 1].start()
    for c in range(CHUNKS):
        load(c, 3).wait()
        cast(g, c, True)

    halo = (
        ((GA0, SA0, RA0), (GB0, SB0, RB0)),
        ((GA1, SA1, RA1), (GB1, SB1, RB1)),
        ((GA2, SA2, RA2), (GB2, SB2, RB2)),
    )
    first = (xi, zi)
    second = (zi, xi)
    even = lax.broadcasted_iota(jnp.int32, (16, LANES), 1) % 2 == 0

    def patch_of(k, one, two, core):
        return two * 8 + one * 2 + core if k == 0 else one * 8 + two * 2 + core

    def spots(k, n):
        z, x, core = n // 8, (n // 2) % 4, n % 2
        return (x, z, core) if k == 0 else (z, x, core)

    def p1_copies(r, k):
        G = halo[r][k][0]
        return [
            rcopy(
                G.at[ci, first[k]], G.at[ci, first[k]], p1_s.at[r, k, d - 1], p1_r.at[r, k, d - 1],
                (g, patch_of(k, (first[k] + d) % 4, second[k], ci)),
            )
            for d in (2, 1, 3)
        ]

    def p2_copy(r, k):
        G = halo[r][k][0]
        return rcopy(
            G.at[ci], G.at[ci], p2_s.at[r, k], p2_r.at[r, k],
            (g, patch_of(k, first[k], second[k], 1 - ci)),
        )

    def p3_copy(r, k, d):
        _, Sd, R = halo[r][k]
        return rcopy(
            Sd.at[d], R.at[second[k]], p3_s.at[r, k, d - 1], p3_r.at[r, k, d - 1],
            (g, patch_of(k, first[k], (second[k] + d) % 4, ci)),
        )

    def put_edge(r, strip, v, value):
        k = 0 if v < SPLIT else 1
        G = halo[r][k][0]
        G[ci, first[k], strip, pl.ds((v - GROUP_VARS[k][0]) * 16, 16), :] = value

    def start_p1(r):
        for k in range(2):
            for copy in p1_copies(r, k):
                copy.start()

    def start_p2(r):
        for k in range(2):
            for copy in p1_copies(r, k):
                copy.wait_recv()
            p2_copy(r, k).start()

    def start_p3(r):
        for k in range(2):
            G, Sd, R = halo[r][k]
            p2_copy(r, k).wait_recv()
            for d in (2, 1, 3, 0):
                t = patch_of(k, first[k], (second[k] + d) % 4, ci)
                at = [spots(k, nbr_ref[j, t]) for j in range(4)]
                north = G[at[0][2], at[0][0], 1]
                south = G[at[1][2], at[1][0], 0]
                if d == 0:
                    R[second[k], 0] = north
                    R[second[k], 1] = south
                else:
                    Sd[d, 0] = north
                    Sd[d, 1] = south
                for v in range(GROUP_ROWS[k] // 16):
                    rows = pl.ds(v * 16, 16)
                    west = G[at[2][2], at[2][0], 2, rows].astype(F32)
                    east = G[at[3][2], at[3][0], 2, rows].astype(F32)
                    mixed = jnp.where(even, east, west).astype(BF16)
                    if d == 0:
                        R[second[k], 2, rows] = mixed
                    else:
                        Sd[d, 2, rows] = mixed
                if d:
                    p3_copy(r, k, d).start()

    def finish_halo(r, T):
        for k in range(2):
            R = halo[r][k][2]
            for d in (2, 1, 3):
                p3_copy(r, k, d).wait_recv()
            at = [spots(k, nbr_ref[j, p])[1] for j in range(4)]
            for v in range(*GROUP_VARS[k]):
                rows = pl.ds((v - GROUP_VARS[k][0]) * 16, 16)
                T[v, :, pl.ds(0, LANES)] = R[at[0], 0, rows].astype(F32)
                T[v, :, pl.ds(LANES + COLS, LANES)] = R[at[1], 1, rows].astype(F32)
                west = pltpu.roll(R[at[2], 2, rows].astype(F32), 1, 1)
                east = pltpu.roll(R[at[3], 2, rows].astype(F32), LANES - 1, 1)
                CB[v] = jnp.where(even, west, east).astype(BF16)

    lane = lax.broadcasted_iota(jnp.int32, (16, LANES), 1)

    def edges(T, r):
        def pick(v, carry):
            acc = jnp.zeros((16, LANES), BF16)
            for x in range(PX):
                mask = (lane == 2 * x) | (lane == (2 * x + LANES - 1) % LANES)
                tile = T[v, :, pl.ds((x + 1) * LANES, LANES)].astype(BF16)
                acc = jnp.where(mask, pltpu.roll(tile, 2 * x, 1), acc)
            EX[v] = acc
            return carry

        lax.fori_loop(0, VARS, pick, 0)
        for v in range(VARS):
            put_edge(r, 0, v, T[v, :, pl.ds(LANES, LANES)].astype(BF16))
            put_edge(r, 1, v, T[v, :, pl.ds(COLS, LANES)].astype(BF16))
            put_edge(r, 2, v, EX[v])

    def substep(T, N, part):
        def step(x, carry):
            here = pl.ds(pl.multiple_of((x + 1) * LANES, LANES), LANES)
            above = pl.ds(pl.multiple_of(x * LANES, LANES), LANES)
            below = pl.ds(pl.multiple_of((x + 2) * LANES, LANES), LANES)
            flat = pl.ds(pl.multiple_of(x * LANES, LANES), LANES)
            hx = HX[:, flat]
            hy = HY[:, flat]
            cn, cs, cw, ce = KAPPA + hx, KAPPA - hx, KAPPA + hy, KAPPA - hy
            for v in range(VARS):
                c = T[v, :, here]
                edge = pltpu.roll(CB[v], (LANES - 2 * x) % LANES, 1).astype(F32)
                w = jnp.where(lane == 0, edge, pltpu.roll(c, 1, 1))
                e = jnp.where(lane == LANES - 1, edge, pltpu.roll(c, LANES - 1, 1))
                N[v, :, here] = (
                    (1.0 - 4.0 * KAPPA) * c
                    + (cn * T[v, :, above] + cs * T[v, :, below])
                    + (cw * w + ce * e)
                )
            return carry

        lax.fori_loop(part * 16, part * 16 + 16, step, 0, unroll=8)

    def halve():
        for copy in cour:
            copy.wait()
        blank = jnp.zeros((1, COLS), F32)
        HX[...] = jnp.concatenate([0.5 * CX[...], blank], axis=0)
        HY[...] = jnp.concatenate([0.5 * CY[...], blank], axis=0)

    def prepare():
        for copy in params[1:]:
            copy.wait()
        j = lax.broadcasted_iota(jnp.int32, (4 * ROWS, 1), 0)
        grp = (j >= ROWS).astype(jnp.int32) + (j >= 2 * ROWS).astype(jnp.int32) + (j >= 3 * ROWS).astype(jnp.int32)
        rest = j - grp * ROWS
        var, lev = rest >> 4, rest & 15
        state_row = var * LEV + grp * SHARE + lev
        surf_row = jnp.where(var < SSHARE, VARS * LEV + grp * SSHARE + var, -1)
        source = jnp.where(lev < SHARE, state_row, surf_row)
        pick = (source == lax.broadcasted_iota(jnp.int32, (4 * ROWS, FEAT), 1)).astype(F32).astype(BF16)
        placed = jnp.dot(pick, w_in[...], preferred_element_type=F32)
        W1[...] = placed.T.astype(BF16)
        source = jnp.where(lev < SHARE, state_row, -1)
        pick = (source == lax.broadcasted_iota(jnp.int32, (4 * ROWS, OUTF), 1)).astype(F32).astype(BF16)
        W2[...] = jnp.dot(pick, w_out[...], preferred_element_type=F32).astype(BF16)
        for i in range(MIDS):
            WM[i] = w_mid[i].astype(F32).T.astype(BF16)
        for i in range(MIDS + 1):
            BB[i] = jnp.broadcast_to(b_hid[i : i + 1, :], (LANES, HID)).T

    def silu(i, pre):
        half = 0.5 * (pre + jnp.concatenate([BB[i]] * (WIDE // LANES), axis=1))
        return (half + half * jnp.tanh(half)).astype(BF16)

    def physics(c):
        whole = pl.ds(c * WIDE, WIDE)
        in_copies(c)[2].wait_recv()
        in_copies(c)[3].wait_recv()
        for copy in in_forwards(c):
            copy.wait_recv()
        hidden = silu(0, jnp.dot(W1[...], X[:, whole], preferred_element_type=F32))
        for i in range(MIDS):
            hidden = silu(i + 1, jnp.dot(WM[i], hidden, preferred_element_type=F32))
        total = jnp.zeros((1, WIDE), F32)
        level = lax.broadcasted_iota(jnp.int32, (16, WIDE), 0)
        for d in range(4):
            tend = jnp.dot(W2[pl.ds(d * ROWS, ROWS)], hidden, preferred_element_type=F32).astype(BF16)
            TO[pl.ds(d * ROWS, ROWS), whole] = tend
            first_var = jnp.where(level < SHARE, tend[:16].astype(F32), 0.0)
            total = total + jnp.sum(first_var, axis=0, keepdims=True)
        total = HEAT_WEIGHT * total
        for i in range(WIDE // LANES):
            HT[pl.ds(c * (WIDE // LANES) + i, 1), :] = total[:, i * LANES : (i + 1) * LANES]
        for copy in out_copies(c):
            copy.start()

    def forward_in(c):
        copies = in_copies(c)
        forwards = in_forwards(c)
        for i in range(2):
            copies[i].wait_recv()
            forwards[i].start()

    def forward_out(c):
        copies = out_copies(c)
        forwards = out_forwards(c)
        for i in range(2):
            copies[i].wait_recv()
            forwards[i].start()

    def z_copy(d):
        z = (zi + d) % 4
        return rcopy(
            PK.at[pl.ds(pl.multiple_of(z * 16, 16), 16)], HZ.at[zi], hz_s.at[d - 1], hz_r.at[d - 1],
            (g, z * 8 + xi * 2 + ci),
        )

    def x_copy(d):
        x = (xi + d) % 4
        return rcopy(
            HZ2.at[x], HXX.at[xi], hx_s.at[d - 1], hx_r.at[d - 1], (g, zi * 8 + x * 2 + ci)
        )

    def c_copy():
        return rcopy(
            HC.at[1 - ci], HR.at[ci], hc_s.at[0], hc_r.at[0], (g, p + 1 - 2 * ci)
        )

    def heat_z():
        owner = [owner_ref[p * PX + g * 16 + b] for b in range(16)]
        slot = []
        for b in range(16):
            rank = jnp.int32(0)
            for before in range(b):
                rank = rank + (owner[before] == owner[b]).astype(jnp.int32)
            slot.append(owner[b] * 2 + rank)
        rows = lax.broadcasted_iota(jnp.int32, (64, LANES), 0)
        table = jnp.zeros((64, LANES), F32)
        for b in range(16):
            table = jnp.where(rows == slot[b], jnp.broadcast_to(HT[pl.ds(b, 1), :], (64, LANES)), table)
        PK[...] = table
        HZ[zi] = PK[pl.ds(pl.multiple_of(zi * 16, 16), 16), :]
        for d in (2, 1, 3):
            z_copy(d).start()

    def heat_x():
        for d in (2, 1, 3):
            z_copy(d).wait_recv()
        for z in range(4):
            for x in range(4):
                HZ2[x, pl.ds(z * 4, 4), :] = HZ[z, pl.ds(x * 4, 4), :]
        HXX[xi] = HZ2[xi]
        for d in (2, 1, 3):
            x_copy(d).start()

    def heat_c():
        for d in (2, 1, 3):
            x_copy(d).wait_recv()
        for c in range(2):
            for z in range(4):
                for x in range(4):
                    HC[c, pl.ds(z * 8 + x * 2, 2), :] = HXX[x, pl.ds(z * 4 + c * 2, 2), :]
        HR[ci] = HC[ci]
        c_copy().start()

    def heat_end():
        c_copy().wait_recv()
        for c in range(2):
            for z in range(4):
                for x in range(4):
                    heat_out[pl.ds(z * 16 + x * 4 + c * 2, 2), :] = HR[c, pl.ds(z * 8 + x * 2, 2), :]

    def finish(c):
        whole = pl.ds(c * WIDE, WIDE)
        for i in (3, 2, 1, 0):
            q = order[i]
            if i == 2:
                out_copies(c)[2].wait_recv()
            elif i == 1:
                out_copies(c)[3].wait_recv()
            elif i == 0:
                for copy in out_forwards(c):
                    copy.wait_recv()
            here = pl.ds(pl.multiple_of(col0(q, c) + LANES, LANES), WIDE)
            for v in range(VARS):
                if i == 3:
                    tend = TO[pl.ds(pl.multiple_of(g * ROWS + v * 16, 16), 16), whole]
                else:
                    tend = TR[q, pl.ds(v * 16, 16), whole]
                total = T1[v, :, here] + PHYS_DT * tend.astype(F32)
                out[v, :, pl.ds(col0(q, c), WIDE)] = total[:SHARE]

    edges(S, 0)
    start_p1(0)
    halve()
    forward_in(0)
    prepare()
    start_p2(0)
    forward_in(1)
    start_p3(0)
    physics(0)
    finish_halo(0, S)
    substep(S, T1, 0)
    substep(S, T1, 1)
    forward_in(2)
    substep(S, T1, 2)
    substep(S, T1, 3)
    edges(T1, 1)
    start_p1(1)
    physics(1)
    start_p2(1)
    forward_in(3)
    forward_out(0)
    start_p3(1)
    physics(2)
    finish_halo(1, T1)
    substep(T1, S, 0)
    substep(T1, S, 1)
    forward_out(1)
    substep(T1, S, 2)
    substep(T1, S, 3)
    edges(S, 2)
    start_p1(2)
    physics(3)
    heat_z()
    start_p2(2)
    forward_out(2)
    start_p3(2)
    heat_x()
    forward_out(3)
    finish_halo(2, S)
    for part in range(4):
        substep(S, T1, part)
    heat_c()
    for c in range(CHUNKS):
        finish(c)
    heat_end()
    for c in range(CHUNKS):
        for copy in in_copies(c) + in_forwards(c) + out_copies(c) + out_forwards(c):
            copy.wait_send()
    for r in range(ROUNDS):
        for k in range(2):
            for copy in p1_copies(r, k):
                copy.wait_send()
            p2_copy(r, k).wait_send()
            for d in (1, 2, 3):
                p3_copy(r, k, d).wait_send()
    for d in (1, 2, 3):
        z_copy(d).wait_send()
        x_copy(d).wait_send()
    c_copy().wait_send()


def on_device(
    state, courant_x, courant_y, surface, w_in, b_hidden, w_mid, w_out, owner_map, neighbours
):
    smem = pl.BlockSpec(memory_space=pltpu.SMEM)
    vmem = pl.BlockSpec(memory_space=pltpu.VMEM)
    anyw = pl.BlockSpec(memory_space=pltpu.HBM)
    dma = pltpu.SemaphoreType.DMA
    padded = pltpu.VMEM((VARS, 16, COLS + 2 * LANES), F32)
    halo_shapes = []
    for lead in ((2, 4, 3), (4, 3), (4, 3)) * ROUNDS:
        for rows in GROUP_ROWS:
            halo_shapes.append(pltpu.VMEM(lead + (rows, LANES), BF16))
    return pl.pallas_call(
        kernel,
        name="couple",
        out_shape=(
            pltpu.VMEM((VARS, SHARE, COLS), F32),
            pltpu.VMEM((64, LANES), F32),
        ),
        in_specs=[smem, smem] + [anyw] * 8,
        out_specs=(vmem, vmem),
        scratch_shapes=[
            pltpu.VMEM((VARS, SHARE, COLS), F32), padded, padded,
            pltpu.VMEM((SHARE, COLS), F32), pltpu.VMEM((SHARE, COLS), F32),
            pltpu.VMEM((16, COLS), F32), pltpu.VMEM((16, COLS), F32),
            pltpu.VMEM((SSHARE, COLS), BF16),
            pltpu.VMEM((FEAT, HID), BF16),
            pltpu.VMEM((MIDS + 1, HID), F32),
            pltpu.VMEM((MIDS, HID, HID), BF16),
            pltpu.VMEM((OUTF, HID), BF16),
            pltpu.VMEM((4, ROWS, QUARTER), BF16),
            pltpu.VMEM((4 * ROWS, QUARTER), BF16),
            pltpu.VMEM((CHUNKS, ROWS, HALF), BF16), pltpu.VMEM((CHUNKS, ROWS, HALF), BF16),
            pltpu.VMEM((4 * ROWS, QUARTER), BF16),
            pltpu.VMEM((4, ROWS, QUARTER), BF16),
            pltpu.VMEM((CHUNKS, ROWS, HALF), BF16), pltpu.VMEM((CHUNKS, ROWS, HALF), BF16),
            pltpu.VMEM((HID, 4 * ROWS), BF16),
            pltpu.VMEM((MIDS, HID, HID), BF16),
            pltpu.VMEM((4 * ROWS, HID), BF16),
            pltpu.VMEM((MIDS + 1, HID, LANES), F32),
            pltpu.VMEM((VARS, 16, LANES), BF16),
            pltpu.VMEM((VARS, 16, LANES), BF16),
            pltpu.VMEM((16, LANES), F32),
            pltpu.VMEM((64, LANES), F32),
            pltpu.VMEM((4, 16, LANES), F32),
            pltpu.VMEM((4, 16, LANES), F32),
            pltpu.VMEM((4, 16, LANES), F32),
            pltpu.VMEM((2, 32, LANES), F32),
            pltpu.VMEM((2, 32, LANES), F32),
            *halo_shapes,
            dma((CHUNKS, 4)), dma((2,)), dma((5,)),
            dma((CHUNKS, 4)), dma((CHUNKS, 4)), dma((CHUNKS, 2)), dma((CHUNKS, 2)),
            dma((CHUNKS, 4)), dma((CHUNKS, 4)), dma((CHUNKS, 2)), dma((CHUNKS, 2)),
            dma((ROUNDS, 2, 3)), dma((ROUNDS, 2, 3)), dma((ROUNDS, 2)), dma((ROUNDS, 2)),
            dma((ROUNDS, 2, 3)), dma((ROUNDS, 2, 3)),
            dma((3,)), dma((3,)), dma((3,)), dma((3,)), dma((1,)), dma((1,)),
        ],
        compiler_params=pltpu.CompilerParams(
            collective_id=0, has_side_effects=True, vmem_limit_bytes=58 * 2**20
        ),
    )(
        owner_map.reshape(-1), neighbours.T, state, courant_x, courant_y, surface,
        w_in, b_hidden, w_mid, w_out.T,
    )


def solution(mesh):
    placed = (
        P(None, "grp", "patch"), P("grp", "patch"), P("grp", "patch"), P("grp", "patch"),
        P(), P(), P(), P(), P(), P(),
    )
    return jax.shard_map(
        on_device,
        mesh=mesh,
        in_specs=placed,
        out_specs=(P(None, "grp", "patch"), P("grp", "patch")),
        check_vma=False,
    )
```

```python
import jax
import jax.numpy as jnp
from jax import lax
from jax.experimental import pallas as pl
from jax.experimental.pallas import tpu as pltpu
from jax.sharding import PartitionSpec as P

MESH = pl.DeviceIdType.MESH
F32 = jnp.float32
BF16 = jnp.bfloat16

VARS = 9
LEV = 60
SHARE = 15
SURF = 16
SSHARE = 4
HID = 256
MIDS = 3
PX = 64
LANES = 128
COLS = PX * LANES
QUARTER = COLS // 4
ROWS = VARS * 16
FEAT = 556
OUTF = 540
CHUNKS = 4
WIDE = QUARTER // CHUNKS
HALF = WIDE // 2
ROUNDS = 3
SPLIT = 5
GROUP_VARS = ((0, SPLIT), (SPLIT, VARS))
GROUP_ROWS = (SPLIT * 16, (VARS - SPLIT) * 16)

KAPPA = 0.24
PHYS_DT = 0.05
HEAT_WEIGHT = 0.125


def kernel(
    owner_ref, nbr_ref, state, courx, coury, surf_in, w_in_in, b_hid_in, w_mid_in, w_out_in,
    out, heat_out,
    ST, S, T1, CX, CY, HX, HY, CK, NS, surf, w_in, b_hid, w_mid, w_out,
    F, X, FP, FM, TO, TR, OP, OM,
    W1, WM, W2, BB, CB, EX, HT, PK, HZ, HZ2, HXX, HC, HR,
    GA0, GB0, SA0, SB0, RA0, RB0, GA1, GB1, SA1, SB1, RA1, RB1, GA2, GB2, SA2, SB2, RA2, RB2,
    load_sem, cour_sem, par_sem,
    in_s, in_r, fw_s, fw_r, out_s, out_r, of_s, of_r,
    p1_s, p1_r, p2_s, p2_r, p3_s, p3_r, hz_s, hz_r, hx_s, hx_r, hc_s, hc_r,
):
    g = lax.axis_index("grp")
    p = lax.axis_index("patch")
    zi, xi, ci = p // 8, (p // 2) % 4, p % 2
    gp, gm, go = (g + 1) % 4, (g + 3) % 4, (g + 2) % 4

    def rcopy(src, dst, ss, rs, dev):
        return pltpu.make_async_remote_copy(
            src_ref=src, dst_ref=dst, send_sem=ss, recv_sem=rs, device_id=dev, device_id_type=MESH
        )

    def col0(q, c):
        return pl.multiple_of(q * QUARTER + c * WIDE, LANES)

    order = (go, gp, gm, g)

    def load(c, i):
        off = col0(order[i], c)
        return pltpu.make_async_copy(
            state.at[:, :, pl.ds(off, WIDE)],
            ST.at[:, :, pl.ds(off, WIDE)],
            load_sem.at[c, i],
        )

    params = tuple(
        pltpu.make_async_copy(src, dst, par_sem.at[i])
        for i, (src, dst) in enumerate(
            ((surf_in, surf), (w_in_in, w_in), (b_hid_in, b_hid), (w_mid_in, w_mid), (w_out_in, w_out))
        )
    )
    cour = (
        pltpu.make_async_copy(courx, CX, cour_sem.at[0]),
        pltpu.make_async_copy(coury, CY, cour_sem.at[1]),
    )

    barrier = pltpu.get_barrier_semaphore()
    for other in (gp, gm, go):
        pl.semaphore_signal(barrier, inc=1, device_id=(other, p), device_id_type=MESH)
    for d in (1, 2, 3):
        pl.semaphore_signal(
            barrier, inc=1, device_id=(g, zi * 8 + ((xi + d) % 4) * 2 + ci), device_id_type=MESH
        )
        pl.semaphore_signal(
            barrier, inc=1, device_id=(g, ((zi + d) % 4) * 8 + xi * 2 + ci), device_id_type=MESH
        )
    pl.semaphore_signal(barrier, inc=1, device_id=(g, p + 1 - 2 * ci), device_id_type=MESH)

    params[0].start()
    for c in range(CHUNKS):
        for i in range(4):
            load(c, i).start()
    for copy in params[1:] + cour:
        copy.start()
    params[0].wait()

    def cast(q, c, own):
        off = col0(q, c)
        here = pl.multiple_of(off + LANES, LANES)
        for v in range(VARS):
            value = ST[v, :, pl.ds(off, WIDE)]
            if v < SSHARE:
                extra = surf[v : v + 1, pl.ds(off, WIDE)].astype(F32)
            else:
                extra = jnp.zeros((1, WIDE), F32)
            value = jnp.concatenate([value, extra], axis=0)
            S[v, :, pl.ds(here, WIDE)] = value
            value = value.astype(BF16)
            if not own:
                F[q, pl.ds(v * 16, 16), pl.ds(c * WIDE, WIDE)] = value
            else:
                X[pl.ds(pl.multiple_of(g * ROWS + v * 16, 16), 16), pl.ds(c * WIDE, WIDE)] = value

    mine = pl.ds(pl.multiple_of(g * ROWS, 16), ROWS)
    prev_rows = pl.ds(pl.multiple_of(gm * ROWS, 16), ROWS)
    next_rows = pl.ds(pl.multiple_of(gp * ROWS, 16), ROWS)
    far_rows = pl.ds(pl.multiple_of(go * ROWS, 16), ROWS)

    def in_copies(c):
        lo, hi, whole = pl.ds(c * WIDE, HALF), pl.ds(c * WIDE + HALF, HALF), pl.ds(c * WIDE, WIDE)
        return (
            rcopy(F.at[go, :, lo], FP.at[c], in_s.at[c, 0], in_r.at[c, 0], (gp, p)),
            rcopy(F.at[go, :, hi], FM.at[c], in_s.at[c, 1], in_r.at[c, 1], (gm, p)),
            rcopy(F.at[gp, :, whole], X.at[mine, whole], in_s.at[c, 2], in_r.at[c, 2], (gp, p)),
            rcopy(F.at[gm, :, whole], X.at[mine, whole], in_s.at[c, 3], in_r.at[c, 3], (gm, p)),
        )

    def in_forwards(c):
        lo, hi = pl.ds(c * WIDE, HALF), pl.ds(c * WIDE + HALF, HALF)
        return (
            rcopy(FP.at[c], X.at[prev_rows, lo], fw_s.at[c, 0], fw_r.at[c, 0], (gp, p)),
            rcopy(FM.at[c], X.at[next_rows, hi], fw_s.at[c, 1], fw_r.at[c, 1], (gm, p)),
        )

    def out_copies(c):
        lo, hi, whole = pl.ds(c * WIDE, HALF), pl.ds(c * WIDE + HALF, HALF), pl.ds(c * WIDE, WIDE)
        return (
            rcopy(TO.at[far_rows, lo], OP.at[c], out_s.at[c, 0], out_r.at[c, 0], (gp, p)),
            rcopy(TO.at[far_rows, hi], OM.at[c], out_s.at[c, 1], out_r.at[c, 1], (gm, p)),
            rcopy(TO.at[next_rows, whole], TR.at[g, :, whole], out_s.at[c, 2], out_r.at[c, 2], (gp, p)),
            rcopy(TO.at[prev_rows, whole], TR.at[g, :, whole], out_s.at[c, 3], out_r.at[c, 3], (gm, p)),
        )

    def out_forwards(c):
        lo, hi = pl.ds(c * WIDE, HALF), pl.ds(c * WIDE + HALF, HALF)
        return (
            rcopy(OP.at[c], TR.at[gm, :, lo], of_s.at[c, 0], of_r.at[c, 0], (gp, p)),
            rcopy(OM.at[c], TR.at[gp, :, hi], of_s.at[c, 1], of_r.at[c, 1], (gm, p)),
        )

    def send_in(c):
        for copy in in_copies(c):
            copy.start()

    for c in range(CHUNKS):
        for i in range(3):
            load(c, i).wait()
            cast(order[i], c, False)
        if c == 0:
            pl.semaphore_wait(barrier, 10)
        if c < 2:
            send_in(c)
    for c in range(CHUNKS):
        load(c, 3).wait()
        cast(g, c, True)

    halo = (
        ((GA0, SA0, RA0), (GB0, SB0, RB0)),
        ((GA1, SA1, RA1), (GB1, SB1, RB1)),
        ((GA2, SA2, RA2), (GB2, SB2, RB2)),
    )
    first = (xi, zi)
    second = (zi, xi)
    even = lax.broadcasted_iota(jnp.int32, (16, LANES), 1) % 2 == 0

    def patch_of(k, one, two, core):
        return two * 8 + one * 2 + core if k == 0 else one * 8 + two * 2 + core

    def spots(k, n):
        z, x, core = n // 8, (n // 2) % 4, n % 2
        return (x, z, core) if k == 0 else (z, x, core)

    def p1_copies(r, k):
        G = halo[r][k][0]
        return [
            rcopy(
                G.at[ci, first[k]], G.at[ci, first[k]], p1_s.at[r, k, d - 1], p1_r.at[r, k, d - 1],
                (g, patch_of(k, (first[k] + d) % 4, second[k], ci)),
            )
            for d in (2, 1, 3)
        ]

    def p2_copy(r, k):
        G = halo[r][k][0]
        return rcopy(
            G.at[ci], G.at[ci], p2_s.at[r, k], p2_r.at[r, k],
            (g, patch_of(k, first[k], second[k], 1 - ci)),
        )

    def p3_copy(r, k, d):
        _, Sd, R = halo[r][k]
        return rcopy(
            Sd.at[d], R.at[second[k]], p3_s.at[r, k, d - 1], p3_r.at[r, k, d - 1],
            (g, patch_of(k, first[k], (second[k] + d) % 4, ci)),
        )

    def put_edge(r, strip, v, value):
        k = 0 if v < SPLIT else 1
        G = halo[r][k][0]
        G[ci, first[k], strip, pl.ds((v - GROUP_VARS[k][0]) * 16, 16), :] = value

    def start_p1(r):
        for k in range(2):
            for copy in p1_copies(r, k):
                copy.start()

    def start_p2(r):
        for k in range(2):
            for copy in p1_copies(r, k):
                copy.wait_recv()
            p2_copy(r, k).start()

    def start_p3(r):
        for k in range(2):
            G, Sd, R = halo[r][k]
            p2_copy(r, k).wait_recv()
            for d in (2, 1, 3, 0):
                t = patch_of(k, first[k], (second[k] + d) % 4, ci)
                at = [spots(k, nbr_ref[j, t]) for j in range(4)]
                north = G[at[0][2], at[0][0], 1]
                south = G[at[1][2], at[1][0], 0]
                if d == 0:
                    R[second[k], 0] = north
                    R[second[k], 1] = south
                else:
                    Sd[d, 0] = north
                    Sd[d, 1] = south
                for v in range(GROUP_ROWS[k] // 16):
                    rows = pl.ds(v * 16, 16)
                    west = G[at[2][2], at[2][0], 2, rows].astype(F32)
                    east = G[at[3][2], at[3][0], 2, rows].astype(F32)
                    mixed = jnp.where(even, east, west).astype(BF16)
                    if d == 0:
                        R[second[k], 2, rows] = mixed
                    else:
                        Sd[d, 2, rows] = mixed
                if d:
                    p3_copy(r, k, d).start()

    def finish_halo(r):
        for k in range(2):
            R = halo[r][k][2]
            for d in (2, 1, 3):
                p3_copy(r, k, d).wait_recv()
            at = [spots(k, nbr_ref[j, p])[1] for j in range(4)]
            for v in range(*GROUP_VARS[k]):
                rows = pl.ds((v - GROUP_VARS[k][0]) * 16, 16)
                NS[v, 0] = R[at[0], 0, rows]
                NS[v, 1] = R[at[1], 1, rows]
                west = pltpu.roll(R[at[2], 2, rows].astype(F32), 1, 1)
                east = pltpu.roll(R[at[3], 2, rows].astype(F32), LANES - 1, 1)
                CB[v] = jnp.where(even, west, east).astype(BF16)

    lane = lax.broadcasted_iota(jnp.int32, (16, LANES), 1)

    def edges(T, r, beside):
        def pick(v, carry):
            acc = jnp.zeros((16, LANES), BF16)
            for x in range(PX):
                here = pl.ds((x + 1) * LANES, LANES)
                tile = T[v, :, here]
                if beside:
                    flat = pl.ds(x * LANES, LANES)
                    side = pltpu.roll(CB[v], (LANES - 2 * x) % LANES, 1).astype(F32)
                    tile = tile + CK[:, flat] * side
                    if x == 0:
                        tile = tile + (KAPPA + HX[:, flat]) * NS[v, 0].astype(F32)
                    if x == PX - 1:
                        tile = tile + (KAPPA - HX[:, flat]) * NS[v, 1].astype(F32)
                    T[v, :, here] = tile
                if r is not None:
                    mask = (lane == 2 * x) | (lane == (2 * x + LANES - 1) % LANES)
                    acc = jnp.where(mask, pltpu.roll(tile.astype(BF16), 2 * x, 1), acc)
            EX[v] = acc
            return carry

        lax.fori_loop(0, VARS, pick, 0)
        if r is None:
            return
        for v in range(VARS):
            put_edge(r, 0, v, T[v, :, pl.ds(LANES, LANES)].astype(BF16))
            put_edge(r, 1, v, T[v, :, pl.ds(COLS, LANES)].astype(BF16))
            put_edge(r, 2, v, EX[v])

    def substep(T, N, part):
        def step(x, carry):
            here = pl.ds(pl.multiple_of((x + 1) * LANES, LANES), LANES)
            above = pl.ds(pl.multiple_of(x * LANES, LANES), LANES)
            below = pl.ds(pl.multiple_of((x + 2) * LANES, LANES), LANES)
            flat = pl.ds(pl.multiple_of(x * LANES, LANES), LANES)
            hx = HX[:, flat]
            hy = HY[:, flat]
            cn, cs = KAPPA + hx, KAPPA - hx
            cw = jnp.where(lane == 0, 0.0, KAPPA + hy)
            ce = jnp.where(lane == LANES - 1, 0.0, KAPPA - hy)
            for v in range(VARS):
                c = T[v, :, here]
                N[v, :, here] = (
                    (1.0 - 4.0 * KAPPA) * c
                    + (cn * T[v, :, above] + cs * T[v, :, below])
                    + (cw * pltpu.roll(c, 1, 1) + ce * pltpu.roll(c, LANES - 1, 1))
                )
            return carry

        lax.fori_loop(part * 16, part * 16 + 16, step, 0, unroll=8)

    def halve():
        for copy in cour:
            copy.wait()
        blank = jnp.zeros((1, COLS), F32)
        HX[...] = jnp.concatenate([0.5 * CX[...], blank], axis=0)
        half = jnp.concatenate([0.5 * CY[...], blank], axis=0)
        HY[...] = half
        place = lax.broadcasted_iota(jnp.int32, (16, COLS), 1) & (LANES - 1)
        CK[...] = jnp.where(
            place == 0, KAPPA + half, jnp.where(place == LANES - 1, KAPPA - half, 0.0)
        )
        for T in (S, T1):
            T[:, :, pl.ds(0, LANES)] = jnp.zeros((VARS, 16, LANES), F32)
            T[:, :, pl.ds(LANES + COLS, LANES)] = jnp.zeros((VARS, 16, LANES), F32)

    def prepare():
        for copy in params[1:]:
            copy.wait()
        j = lax.broadcasted_iota(jnp.int32, (4 * ROWS, 1), 0)
        grp = (j >= ROWS).astype(jnp.int32) + (j >= 2 * ROWS).astype(jnp.int32) + (j >= 3 * ROWS).astype(jnp.int32)
        rest = j - grp * ROWS
        var, lev = rest >> 4, rest & 15
        state_row = var * LEV + grp * SHARE + lev
        surf_row = jnp.where(var < SSHARE, VARS * LEV + grp * SSHARE + var, -1)
        source = jnp.where(lev < SHARE, state_row, surf_row)
        pick = (source == lax.broadcasted_iota(jnp.int32, (4 * ROWS, FEAT), 1)).astype(F32).astype(BF16)
        placed = jnp.dot(pick, w_in[...], preferred_element_type=F32)
        W1[...] = placed.T.astype(BF16)
        source = jnp.where(lev < SHARE, state_row, -1)
        pick = (source == lax.broadcasted_iota(jnp.int32, (4 * ROWS, OUTF), 1)).astype(F32).astype(BF16)
        W2[...] = jnp.dot(pick, w_out[...], preferred_element_type=F32).astype(BF16)
        for i in range(MIDS):
            WM[i] = w_mid[i].astype(F32).T.astype(BF16)
        for i in range(MIDS + 1):
            BB[i] = jnp.broadcast_to(b_hid[i : i + 1, :], (LANES, HID)).T

    def silu(i, pre):
        half = 0.5 * (pre + jnp.concatenate([BB[i]] * (WIDE // LANES), axis=1))
        return (half + half * jnp.tanh(half)).astype(BF16)

    def physics(c):
        whole = pl.ds(c * WIDE, WIDE)
        in_copies(c)[2].wait_recv()
        in_copies(c)[3].wait_recv()
        for copy in in_forwards(c):
            copy.wait_recv()
        hidden = silu(0, jnp.dot(W1[...], X[:, whole], preferred_element_type=F32))
        for i in range(MIDS):
            hidden = silu(i + 1, jnp.dot(WM[i], hidden, preferred_element_type=F32))
        total = jnp.zeros((1, WIDE), F32)
        level = lax.broadcasted_iota(jnp.int32, (16, WIDE), 0)
        for d in range(4):
            tend = jnp.dot(W2[pl.ds(d * ROWS, ROWS)], hidden, preferred_element_type=F32).astype(BF16)
            TO[pl.ds(d * ROWS, ROWS), whole] = tend
            first_var = jnp.where(level < SHARE, tend[:16].astype(F32), 0.0)
            total = total + jnp.sum(first_var, axis=0, keepdims=True)
        total = HEAT_WEIGHT * total
        for i in range(WIDE // LANES):
            HT[pl.ds(c * (WIDE // LANES) + i, 1), :] = total[:, i * LANES : (i + 1) * LANES]
        for copy in out_copies(c):
            copy.start()

    def forward_in(c):
        copies = in_copies(c)
        forwards = in_forwards(c)
        for i in range(2):
            copies[i].wait_recv()
            forwards[i].start()

    def forward_out(c):
        copies = out_copies(c)
        forwards = out_forwards(c)
        for i in range(2):
            copies[i].wait_recv()
            forwards[i].start()

    def z_copy(d):
        z = (zi + d) % 4
        return rcopy(
            PK.at[pl.ds(pl.multiple_of(z * 16, 16), 16)], HZ.at[zi], hz_s.at[d - 1], hz_r.at[d - 1],
            (g, z * 8 + xi * 2 + ci),
        )

    def x_copy(d):
        x = (xi + d) % 4
        return rcopy(
            HZ2.at[x], HXX.at[xi], hx_s.at[d - 1], hx_r.at[d - 1], (g, zi * 8 + x * 2 + ci)
        )

    def c_copy():
        return rcopy(
            HC.at[1 - ci], HR.at[ci], hc_s.at[0], hc_r.at[0], (g, p + 1 - 2 * ci)
        )

    def heat_z():
        owner = [owner_ref[p * PX + g * 16 + b] for b in range(16)]
        slot = []
        for b in range(16):
            rank = jnp.int32(0)
            for before in range(b):
                rank = rank + (owner[before] == owner[b]).astype(jnp.int32)
            slot.append(owner[b] * 2 + rank)
        rows = lax.broadcasted_iota(jnp.int32, (64, LANES), 0)
        table = jnp.zeros((64, LANES), F32)
        for b in range(16):
            table = jnp.where(rows == slot[b], jnp.broadcast_to(HT[pl.ds(b, 1), :], (64, LANES)), table)
        PK[...] = table
        HZ[zi] = PK[pl.ds(pl.multiple_of(zi * 16, 16), 16), :]
        for d in (2, 1, 3):
            z_copy(d).start()

    def heat_x():
        for d in (2, 1, 3):
            z_copy(d).wait_recv()
        for z in range(4):
            for x in range(4):
                HZ2[x, pl.ds(z * 4, 4), :] = HZ[z, pl.ds(x * 4, 4), :]
        HXX[xi] = HZ2[xi]
        for d in (2, 1, 3):
            x_copy(d).start()

    def heat_c():
        for d in (2, 1, 3):
            x_copy(d).wait_recv()
        for c in range(2):
            for z in range(4):
                for x in range(4):
                    HC[c, pl.ds(z * 8 + x * 2, 2), :] = HXX[x, pl.ds(z * 4 + c * 2, 2), :]
        HR[ci] = HC[ci]
        c_copy().start()

    def heat_end():
        c_copy().wait_recv()
        for c in range(2):
            for z in range(4):
                for x in range(4):
                    heat_out[pl.ds(z * 16 + x * 4 + c * 2, 2), :] = HR[c, pl.ds(z * 8 + x * 2, 2), :]

    def finish(c):
        whole = pl.ds(c * WIDE, WIDE)
        for i in (3, 2, 1, 0):
            q = order[i]
            if i == 2:
                out_copies(c)[2].wait_recv()
            elif i == 1:
                out_copies(c)[3].wait_recv()
            elif i == 0:
                for copy in out_forwards(c):
                    copy.wait_recv()
            here = pl.ds(pl.multiple_of(col0(q, c) + LANES, LANES), WIDE)
            for v in range(VARS):
                if i == 3:
                    tend = TO[pl.ds(pl.multiple_of(g * ROWS + v * 16, 16), 16), whole]
                else:
                    tend = TR[q, pl.ds(v * 16, 16), whole]
                total = T1[v, :, here] + PHYS_DT * tend.astype(F32)
                out[v, :, pl.ds(col0(q, c), WIDE)] = total[:SHARE]

    edges(S, 0, False)
    start_p1(0)
    forward_in(0)
    send_in(2)
    halve()
    start_p2(0)
    prepare()
    forward_in(1)
    start_p3(0)
    send_in(3)
    substep(S, T1, 0)
    substep(S, T1, 1)
    physics(0)
    substep(S, T1, 2)
    substep(S, T1, 3)
    finish_halo(0)
    edges(T1, 1, True)
    start_p1(1)
    forward_in(2)
    substep(T1, S, 0)
    substep(T1, S, 1)
    start_p2(1)
    physics(1)
    start_p3(1)
    forward_in(3)
    forward_out(0)
    substep(T1, S, 2)
    substep(T1, S, 3)
    finish_halo(1)
    edges(S, 2, True)
    start_p1(2)
    physics(2)
    start_p2(2)
    forward_out(1)
    physics(3)
    start_p3(2)
    heat_z()
    substep(S, T1, 0)
    substep(S, T1, 1)
    forward_out(2)
    heat_x()
    substep(S, T1, 2)
    substep(S, T1, 3)
    heat_c()
    finish_halo(2)
    forward_out(3)
    edges(T1, None, True)
    for c in range(CHUNKS):
        finish(c)
    heat_end()
    for c in range(CHUNKS):
        for copy in in_copies(c) + in_forwards(c) + out_copies(c) + out_forwards(c):
            copy.wait_send()
    for r in range(ROUNDS):
        for k in range(2):
            for copy in p1_copies(r, k):
                copy.wait_send()
            p2_copy(r, k).wait_send()
            for d in (1, 2, 3):
                p3_copy(r, k, d).wait_send()
    for d in (1, 2, 3):
        z_copy(d).wait_send()
        x_copy(d).wait_send()
    c_copy().wait_send()


def on_device(
    state, courant_x, courant_y, surface, w_in, b_hidden, w_mid, w_out, owner_map, neighbours
):
    smem = pl.BlockSpec(memory_space=pltpu.SMEM)
    vmem = pl.BlockSpec(memory_space=pltpu.VMEM)
    anyw = pl.BlockSpec(memory_space=pltpu.HBM)
    dma = pltpu.SemaphoreType.DMA
    padded = pltpu.VMEM((VARS, 16, COLS + 2 * LANES), F32)
    halo_shapes = []
    for lead in ((2, 4, 3), (4, 3), (4, 3)) * ROUNDS:
        for rows in GROUP_ROWS:
            halo_shapes.append(pltpu.VMEM(lead + (rows, LANES), BF16))
    return pl.pallas_call(
        kernel,
        name="couple",
        out_shape=(
            pltpu.VMEM((VARS, SHARE, COLS), F32),
            pltpu.VMEM((64, LANES), F32),
        ),
        in_specs=[smem, smem] + [anyw] * 8,
        out_specs=(vmem, vmem),
        scratch_shapes=[
            pltpu.VMEM((VARS, SHARE, COLS), F32), padded, padded,
            pltpu.VMEM((SHARE, COLS), F32), pltpu.VMEM((SHARE, COLS), F32),
            pltpu.VMEM((16, COLS), F32), pltpu.VMEM((16, COLS), F32),
            pltpu.VMEM((16, COLS), F32), pltpu.VMEM((VARS, 2, 16, LANES), BF16),
            pltpu.VMEM((SSHARE, COLS), BF16),
            pltpu.VMEM((FEAT, HID), BF16),
            pltpu.VMEM((MIDS + 1, HID), F32),
            pltpu.VMEM((MIDS, HID, HID), BF16),
            pltpu.VMEM((OUTF, HID), BF16),
            pltpu.VMEM((4, ROWS, QUARTER), BF16),
            pltpu.VMEM((4 * ROWS, QUARTER), BF16),
            pltpu.VMEM((CHUNKS, ROWS, HALF), BF16), pltpu.VMEM((CHUNKS, ROWS, HALF), BF16),
            pltpu.VMEM((4 * ROWS, QUARTER), BF16),
            pltpu.VMEM((4, ROWS, QUARTER), BF16),
            pltpu.VMEM((CHUNKS, ROWS, HALF), BF16), pltpu.VMEM((CHUNKS, ROWS, HALF), BF16),
            pltpu.VMEM((HID, 4 * ROWS), BF16),
            pltpu.VMEM((MIDS, HID, HID), BF16),
            pltpu.VMEM((4 * ROWS, HID), BF16),
            pltpu.VMEM((MIDS + 1, HID, LANES), F32),
            pltpu.VMEM((VARS, 16, LANES), BF16),
            pltpu.VMEM((VARS, 16, LANES), BF16),
            pltpu.VMEM((16, LANES), F32),
            pltpu.VMEM((64, LANES), F32),
            pltpu.VMEM((4, 16, LANES), F32),
            pltpu.VMEM((4, 16, LANES), F32),
            pltpu.VMEM((4, 16, LANES), F32),
            pltpu.VMEM((2, 32, LANES), F32),
            pltpu.VMEM((2, 32, LANES), F32),
            *halo_shapes,
            dma((CHUNKS, 4)), dma((2,)), dma((5,)),
            dma((CHUNKS, 4)), dma((CHUNKS, 4)), dma((CHUNKS, 2)), dma((CHUNKS, 2)),
            dma((CHUNKS, 4)), dma((CHUNKS, 4)), dma((CHUNKS, 2)), dma((CHUNKS, 2)),
            dma((ROUNDS, 2, 3)), dma((ROUNDS, 2, 3)), dma((ROUNDS, 2)), dma((ROUNDS, 2)),
            dma((ROUNDS, 2, 3)), dma((ROUNDS, 2, 3)),
            dma((3,)), dma((3,)), dma((3,)), dma((3,)), dma((1,)), dma((1,)),
        ],
        compiler_params=pltpu.CompilerParams(
            collective_id=0, has_side_effects=True, vmem_limit_bytes=58 * 2**20
        ),
    )(
        owner_map.reshape(-1), neighbours.T, state, courant_x, courant_y, surface,
        w_in, b_hidden, w_mid, w_out.T,
    )


def solution(mesh):
    placed = (
        P(None, "grp", "patch"), P("grp", "patch"), P("grp", "patch"), P("grp", "patch"),
        P(), P(), P(), P(), P(), P(),
    )
    return jax.shard_map(
        on_device,
        mesh=mesh,
        in_specs=placed,
        out_specs=(P(None, "grp", "patch"), P("grp", "patch")),
        check_vma=False,
    )
```

```python
import jax
import jax.numpy as jnp
from jax import lax
from jax.experimental import pallas as pl
from jax.experimental.pallas import tpu as pltpu
from jax.sharding import PartitionSpec as P

MESH = pl.DeviceIdType.MESH
F32 = jnp.float32
BF16 = jnp.bfloat16

VARS = 9
LEV = 60
SHARE = 15
SURF = 16
SSHARE = 4
HID = 256
MIDS = 3
PX = 64
LANES = 128
COLS = PX * LANES
QUARTER = COLS // 4
ROWS = VARS * 16
OROWS = 136
FEAT = 556
OUTF = 540
CHUNKS = 4
WIDE = QUARTER // CHUNKS
HALF = WIDE // 2
ROUNDS = 3
SPLIT = 5
GROUP_VARS = ((0, SPLIT), (SPLIT, VARS))
GROUP_ROWS = (SPLIT * 16, (VARS - SPLIT) * 16)

KAPPA = 0.24
PHYS_DT = 0.05
HEAT_WEIGHT = 0.125


def kernel(
    owner_ref, nbr_ref, state, courx, coury, surf_in, w_in_in, b_hid_in, w_mid_in, w_out_in,
    out, heat_out,
    ST, S, T1, CX, CY, HX, HY, CK, NS, surf, w_in, b_hid, w_mid, w_out,
    F, X, FP, FM, TN, TF, RN, RF, OP, OM,
    W1, WM, W2, BB, CB, EX, HT, PK, HZ, HZ2, HXX, HC, HR,
    GA0, GB0, SA0, SB0, RA0, RB0, GA1, GB1, SA1, SB1, RA1, RB1, GA2, GB2, SA2, SB2, RA2, RB2,
    load_sem, cour_sem, par_sem,
    in_s, in_r, fw_s, fw_r, out_s, out_r, of_s, of_r,
    p1_s, p1_r, p2_s, p2_r, p3_s, p3_r, hz_s, hz_r, hx_s, hx_r, hc_s, hc_r,
):
    g = lax.axis_index("grp")
    p = lax.axis_index("patch")
    zi, xi, ci = p // 8, (p // 2) % 4, p % 2
    gp, gm, go = (g + 1) % 4, (g + 3) % 4, (g + 2) % 4

    def rcopy(src, dst, ss, rs, dev):
        return pltpu.make_async_remote_copy(
            src_ref=src, dst_ref=dst, send_sem=ss, recv_sem=rs, device_id=dev, device_id_type=MESH
        )

    def col0(q, c):
        return pl.multiple_of(q * QUARTER + c * WIDE, LANES)

    order = (go, gp, gm, g)

    def load(c, i):
        off = col0(order[i], c)
        return pltpu.make_async_copy(
            state.at[:, :, pl.ds(off, WIDE)],
            ST.at[:, :, pl.ds(off, WIDE)],
            load_sem.at[c, i],
        )

    params = tuple(
        pltpu.make_async_copy(src, dst, par_sem.at[i])
        for i, (src, dst) in enumerate(
            ((surf_in, surf), (w_in_in, w_in), (b_hid_in, b_hid), (w_mid_in, w_mid), (w_out_in, w_out))
        )
    )
    cour = (
        pltpu.make_async_copy(courx, CX, cour_sem.at[0]),
        pltpu.make_async_copy(coury, CY, cour_sem.at[1]),
    )

    barrier = pltpu.get_barrier_semaphore()
    for other in (gp, gm, go):
        pl.semaphore_signal(barrier, inc=1, device_id=(other, p), device_id_type=MESH)
    for d in (1, 2, 3):
        pl.semaphore_signal(
            barrier, inc=1, device_id=(g, zi * 8 + ((xi + d) % 4) * 2 + ci), device_id_type=MESH
        )
        pl.semaphore_signal(
            barrier, inc=1, device_id=(g, ((zi + d) % 4) * 8 + xi * 2 + ci), device_id_type=MESH
        )
    pl.semaphore_signal(barrier, inc=1, device_id=(g, p + 1 - 2 * ci), device_id_type=MESH)

    params[0].start()
    for c in range(CHUNKS):
        for i in range(4):
            load(c, i).start()
    for copy in params[1:] + cour:
        copy.start()
    params[0].wait()

    def cast(q, c, own):
        off = col0(q, c)
        here = pl.multiple_of(off + LANES, LANES)
        for v in range(VARS):
            value = ST[v, :, pl.ds(off, WIDE)]
            if v < SSHARE:
                extra = surf[v : v + 1, pl.ds(off, WIDE)].astype(F32)
            else:
                extra = jnp.zeros((1, WIDE), F32)
            value = jnp.concatenate([value, extra], axis=0)
            S[v, :, pl.ds(here, WIDE)] = value
            value = value.astype(BF16)
            if not own:
                F[q, pl.ds(v * 16, 16), pl.ds(c * WIDE, WIDE)] = value
            else:
                X[pl.ds(pl.multiple_of(g * ROWS + v * 16, 16), 16), pl.ds(c * WIDE, WIDE)] = value

    mine = pl.ds(pl.multiple_of(g * ROWS, 16), ROWS)
    prev_rows = pl.ds(pl.multiple_of(gm * ROWS, 16), ROWS)
    next_rows = pl.ds(pl.multiple_of(gp * ROWS, 16), ROWS)

    def in_copies(c):
        lo, hi, whole = pl.ds(c * WIDE, HALF), pl.ds(c * WIDE + HALF, HALF), pl.ds(c * WIDE, WIDE)
        return (
            rcopy(F.at[go, :, lo], FP.at[c], in_s.at[c, 0], in_r.at[c, 0], (gp, p)),
            rcopy(F.at[go, :, hi], FM.at[c], in_s.at[c, 1], in_r.at[c, 1], (gm, p)),
            rcopy(F.at[gp, :, whole], X.at[mine, whole], in_s.at[c, 2], in_r.at[c, 2], (gp, p)),
            rcopy(F.at[gm, :, whole], X.at[mine, whole], in_s.at[c, 3], in_r.at[c, 3], (gm, p)),
        )

    def in_forwards(c):
        lo, hi = pl.ds(c * WIDE, HALF), pl.ds(c * WIDE + HALF, HALF)
        return (
            rcopy(FP.at[c], X.at[prev_rows, lo], fw_s.at[c, 0], fw_r.at[c, 0], (gp, p)),
            rcopy(FM.at[c], X.at[next_rows, hi], fw_s.at[c, 1], fw_r.at[c, 1], (gm, p)),
        )

    def out_copies(c):
        return (
            rcopy(TF.at[c, 0], OP.at[c], out_s.at[c, 0], out_r.at[c, 0], (gp, p)),
            rcopy(TF.at[c, 1], OM.at[c], out_s.at[c, 1], out_r.at[c, 1], (gm, p)),
            rcopy(TN.at[0, c], RN.at[0, c], out_s.at[c, 2], out_r.at[c, 2], (gp, p)),
            rcopy(TN.at[1, c], RN.at[1, c], out_s.at[c, 3], out_r.at[c, 3], (gm, p)),
        )

    def out_forwards(c):
        return (
            rcopy(OP.at[c], RF.at[0, c], of_s.at[c, 0], of_r.at[c, 0], (gp, p)),
            rcopy(OM.at[c], RF.at[1, c], of_s.at[c, 1], of_r.at[c, 1], (gm, p)),
        )

    def send_in(c):
        for copy in in_copies(c):
            copy.start()

    for c in range(CHUNKS):
        for i in range(3):
            load(c, i).wait()
            cast(order[i], c, False)
        if c == 0:
            pl.semaphore_wait(barrier, 10)
        if c < 2:
            send_in(c)
    for c in range(CHUNKS):
        load(c, 3).wait()
        cast(g, c, True)

    halo = (
        ((GA0, SA0, RA0), (GB0, SB0, RB0)),
        ((GA1, SA1, RA1), (GB1, SB1, RB1)),
        ((GA2, SA2, RA2), (GB2, SB2, RB2)),
    )
    first = (xi, zi)
    second = (zi, xi)
    even = lax.broadcasted_iota(jnp.int32, (16, LANES), 1) % 2 == 0

    def patch_of(k, one, two, core):
        return two * 8 + one * 2 + core if k == 0 else one * 8 + two * 2 + core

    def spots(k, n):
        z, x, core = n // 8, (n // 2) % 4, n % 2
        return (x, z, core) if k == 0 else (z, x, core)

    def p1_copies(r, k):
        G = halo[r][k][0]
        return [
            rcopy(
                G.at[ci, first[k]], G.at[ci, first[k]], p1_s.at[r, k, d - 1], p1_r.at[r, k, d - 1],
                (g, patch_of(k, (first[k] + d) % 4, second[k], ci)),
            )
            for d in (2, 1, 3)
        ]

    def p2_copy(r, k):
        G = halo[r][k][0]
        return rcopy(
            G.at[ci], G.at[ci], p2_s.at[r, k], p2_r.at[r, k],
            (g, patch_of(k, first[k], second[k], 1 - ci)),
        )

    def p3_copy(r, k, d):
        _, Sd, R = halo[r][k]
        return rcopy(
            Sd.at[d], R.at[second[k]], p3_s.at[r, k, d - 1], p3_r.at[r, k, d - 1],
            (g, patch_of(k, first[k], (second[k] + d) % 4, ci)),
        )

    def put_edge(r, strip, v, value):
        k = 0 if v < SPLIT else 1
        G = halo[r][k][0]
        G[ci, first[k], strip, pl.ds((v - GROUP_VARS[k][0]) * 16, 16), :] = value

    def start_p1(r):
        for k in range(2):
            for copy in p1_copies(r, k):
                copy.start()

    def start_p2(r):
        for k in range(2):
            for copy in p1_copies(r, k):
                copy.wait_recv()
            p2_copy(r, k).start()

    def start_p3(r):
        for k in range(2):
            G, Sd, R = halo[r][k]
            p2_copy(r, k).wait_recv()
            for d in (2, 1, 3, 0):
                t = patch_of(k, first[k], (second[k] + d) % 4, ci)
                at = [spots(k, nbr_ref[j, t]) for j in range(4)]
                north = G[at[0][2], at[0][0], 1]
                south = G[at[1][2], at[1][0], 0]
                if d == 0:
                    R[second[k], 0] = north
                    R[second[k], 1] = south
                else:
                    Sd[d, 0] = north
                    Sd[d, 1] = south
                for v in range(GROUP_ROWS[k] // 16):
                    rows = pl.ds(v * 16, 16)
                    west = G[at[2][2], at[2][0], 2, rows].astype(F32)
                    east = G[at[3][2], at[3][0], 2, rows].astype(F32)
                    mixed = jnp.where(even, east, west).astype(BF16)
                    if d == 0:
                        R[second[k], 2, rows] = mixed
                    else:
                        Sd[d, 2, rows] = mixed
                if d:
                    p3_copy(r, k, d).start()

    def finish_halo(r):
        for k in range(2):
            R = halo[r][k][2]
            for d in (2, 1, 3):
                p3_copy(r, k, d).wait_recv()
            at = [spots(k, nbr_ref[j, p])[1] for j in range(4)]
            for v in range(*GROUP_VARS[k]):
                rows = pl.ds((v - GROUP_VARS[k][0]) * 16, 16)
                NS[v, 0] = R[at[0], 0, rows]
                NS[v, 1] = R[at[1], 1, rows]
                west = pltpu.roll(R[at[2], 2, rows].astype(F32), 1, 1)
                east = pltpu.roll(R[at[3], 2, rows].astype(F32), LANES - 1, 1)
                CB[v] = jnp.where(even, west, east).astype(BF16)

    lane = lax.broadcasted_iota(jnp.int32, (16, LANES), 1)

    def edges(T, r, beside):
        def pick(v, carry):
            acc = jnp.zeros((16, LANES), BF16)
            for x in range(PX):
                here = pl.ds((x + 1) * LANES, LANES)
                tile = T[v, :, here]
                if beside:
                    flat = pl.ds(x * LANES, LANES)
                    side = pltpu.roll(CB[v], (LANES - 2 * x) % LANES, 1).astype(F32)
                    tile = tile + CK[:, flat] * side
                    if x == 0:
                        tile = tile + (KAPPA + HX[:, flat]) * NS[v, 0].astype(F32)
                    if x == PX - 1:
                        tile = tile + (KAPPA - HX[:, flat]) * NS[v, 1].astype(F32)
                    T[v, :, here] = tile
                if r is not None:
                    mask = (lane == 2 * x) | (lane == (2 * x + LANES - 1) % LANES)
                    acc = jnp.where(mask, pltpu.roll(tile.astype(BF16), 2 * x, 1), acc)
            EX[v] = acc
            return carry

        lax.fori_loop(0, VARS, pick, 0)
        if r is None:
            return
        for v in range(VARS):
            put_edge(r, 0, v, T[v, :, pl.ds(LANES, LANES)].astype(BF16))
            put_edge(r, 1, v, T[v, :, pl.ds(COLS, LANES)].astype(BF16))
            put_edge(r, 2, v, EX[v])

    def substep(T, N, part):
        def step(x, carry):
            here = pl.ds(pl.multiple_of((x + 1) * LANES, LANES), LANES)
            above = pl.ds(pl.multiple_of(x * LANES, LANES), LANES)
            below = pl.ds(pl.multiple_of((x + 2) * LANES, LANES), LANES)
            flat = pl.ds(pl.multiple_of(x * LANES, LANES), LANES)
            hx = HX[:, flat]
            hy = HY[:, flat]
            cn, cs = KAPPA + hx, KAPPA - hx
            cw = jnp.where(lane == 0, 0.0, KAPPA + hy)
            ce = jnp.where(lane == LANES - 1, 0.0, KAPPA - hy)
            for v in range(VARS):
                c = T[v, :, here]
                N[v, :, here] = (
                    (1.0 - 4.0 * KAPPA) * c
                    + (cn * T[v, :, above] + cs * T[v, :, below])
                    + (cw * pltpu.roll(c, 1, 1) + ce * pltpu.roll(c, LANES - 1, 1))
                )
            return carry

        lax.fori_loop(part * 16, part * 16 + 16, step, 0, unroll=8)

    def halve():
        for copy in cour:
            copy.wait()
        blank = jnp.zeros((1, COLS), F32)
        HX[...] = jnp.concatenate([0.5 * CX[...], blank], axis=0)
        half = jnp.concatenate([0.5 * CY[...], blank], axis=0)
        HY[...] = half
        place = lax.broadcasted_iota(jnp.int32, (16, COLS), 1) & (LANES - 1)
        CK[...] = jnp.where(
            place == 0, KAPPA + half, jnp.where(place == LANES - 1, KAPPA - half, 0.0)
        )
        for T in (S, T1):
            T[:, :, pl.ds(0, LANES)] = jnp.zeros((VARS, 16, LANES), F32)
            T[:, :, pl.ds(LANES + COLS, LANES)] = jnp.zeros((VARS, 16, LANES), F32)

    def prepare():
        for copy in params[1:]:
            copy.wait()
        j = lax.broadcasted_iota(jnp.int32, (4 * ROWS, 1), 0)
        grp = (j >= ROWS).astype(jnp.int32) + (j >= 2 * ROWS).astype(jnp.int32) + (j >= 3 * ROWS).astype(jnp.int32)
        rest = j - grp * ROWS
        var, lev = rest >> 4, rest & 15
        state_row = var * LEV + grp * SHARE + lev
        surf_row = jnp.where(var < SSHARE, VARS * LEV + grp * SSHARE + var, -1)
        source = jnp.where(lev < SHARE, state_row, surf_row)
        pick = (source == lax.broadcasted_iota(jnp.int32, (4 * ROWS, FEAT), 1)).astype(F32).astype(BF16)
        placed = jnp.dot(pick, w_in[...], preferred_element_type=F32)
        W1[...] = placed.T.astype(BF16)
        j = lax.broadcasted_iota(jnp.int32, (4 * OROWS, 1), 0)
        grp = (j >= OROWS).astype(jnp.int32) + (j >= 2 * OROWS).astype(jnp.int32) + (j >= 3 * OROWS).astype(jnp.int32)
        rest = j - grp * OROWS
        var, lev = rest >> 4, rest & 15
        last = (VARS - 1) * LEV + grp * SHARE
        main_row = jnp.where(lev < SHARE, var * LEV + grp * SHARE + lev, last + var)
        tail_row = jnp.where(rest < OROWS - 1, last + rest - 120, -1)
        source = jnp.where(rest < 128, main_row, tail_row)
        pick = (source == lax.broadcasted_iota(jnp.int32, (4 * OROWS, OUTF), 1)).astype(F32).astype(BF16)
        placed = jnp.dot(pick, w_out[...], preferred_element_type=F32)
        for d in range(4):
            W2[d] = placed[d * OROWS : (d + 1) * OROWS].astype(BF16)
        for i in range(MIDS):
            WM[i] = w_mid[i].astype(F32).T.astype(BF16)
        for i in range(MIDS + 1):
            BB[i] = jnp.broadcast_to(b_hid[i : i + 1, :], (LANES, HID)).T

    def silu(i, pre):
        half = 0.5 * (pre + jnp.concatenate([BB[i]] * (WIDE // LANES), axis=1))
        return (half + half * jnp.tanh(half)).astype(BF16)

    def physics(c):
        whole = pl.ds(c * WIDE, WIDE)
        in_copies(c)[2].wait_recv()
        in_copies(c)[3].wait_recv()
        for copy in in_forwards(c):
            copy.wait_recv()
        hidden = silu(0, jnp.dot(W1[...], X[:, whole], preferred_element_type=F32))
        for i in range(MIDS):
            hidden = silu(i + 1, jnp.dot(WM[i], hidden, preferred_element_type=F32))
        total = jnp.zeros((1, WIDE), F32)
        level = lax.broadcasted_iota(jnp.int32, (16, WIDE), 0)
        def pack(ref, tend):
            n = tend.shape[1] // 2
            ref[pl.ds(0, 128), :] = tend[:128, :n].astype(BF16)
            ref[pl.ds(128, 128), :] = tend[:128, n:].astype(BF16)
            ref[pl.ds(256, 16), :] = jnp.concatenate([tend[128:, :n], tend[128:, n:]], axis=0).astype(BF16)

        for i, d in enumerate((gp, gm, g, go)):
            tend = jnp.dot(W2[d], hidden, preferred_element_type=F32)
            if i < 3:
                pack(TN.at[i, c], tend)
            else:
                pack(TF.at[c, 0], tend[:, :HALF])
                pack(TF.at[c, 1], tend[:, HALF:])
            first_var = jnp.where(level < SHARE, tend[:16].astype(BF16).astype(F32), 0.0)
            total = total + jnp.sum(first_var, axis=0, keepdims=True)
        total = HEAT_WEIGHT * total
        for i in range(WIDE // LANES):
            HT[pl.ds(c * (WIDE // LANES) + i, 1), :] = total[:, i * LANES : (i + 1) * LANES]
        for copy in out_copies(c):
            copy.start()

    def forward_in(c):
        copies = in_copies(c)
        forwards = in_forwards(c)
        for i in range(2):
            copies[i].wait_recv()
            forwards[i].start()

    def forward_out(c):
        copies = out_copies(c)
        forwards = out_forwards(c)
        for i in range(2):
            copies[i].wait_recv()
            forwards[i].start()

    def z_copy(d):
        z = (zi + d) % 4
        return rcopy(
            PK.at[pl.ds(pl.multiple_of(z * 16, 16), 16)], HZ.at[zi], hz_s.at[d - 1], hz_r.at[d - 1],
            (g, z * 8 + xi * 2 + ci),
        )

    def x_copy(d):
        x = (xi + d) % 4
        return rcopy(
            HZ2.at[x], HXX.at[xi], hx_s.at[d - 1], hx_r.at[d - 1], (g, zi * 8 + x * 2 + ci)
        )

    def c_copy():
        return rcopy(
            HC.at[1 - ci], HR.at[ci], hc_s.at[0], hc_r.at[0], (g, p + 1 - 2 * ci)
        )

    def heat_z():
        owner = [owner_ref[p * PX + g * 16 + b] for b in range(16)]
        slot = []
        for b in range(16):
            rank = jnp.int32(0)
            for before in range(b):
                rank = rank + (owner[before] == owner[b]).astype(jnp.int32)
            slot.append(owner[b] * 2 + rank)
        rows = lax.broadcasted_iota(jnp.int32, (64, LANES), 0)
        table = jnp.zeros((64, LANES), F32)
        for b in range(16):
            table = jnp.where(rows == slot[b], jnp.broadcast_to(HT[pl.ds(b, 1), :], (64, LANES)), table)
        PK[...] = table
        HZ[zi] = PK[pl.ds(pl.multiple_of(zi * 16, 16), 16), :]
        for d in (2, 1, 3):
            z_copy(d).start()

    def heat_x():
        for d in (2, 1, 3):
            z_copy(d).wait_recv()
        for z in range(4):
            for x in range(4):
                HZ2[x, pl.ds(z * 4, 4), :] = HZ[z, pl.ds(x * 4, 4), :]
        HXX[xi] = HZ2[xi]
        for d in (2, 1, 3):
            x_copy(d).start()

    def heat_c():
        for d in (2, 1, 3):
            x_copy(d).wait_recv()
        for c in range(2):
            for z in range(4):
                for x in range(4):
                    HC[c, pl.ds(z * 8 + x * 2, 2), :] = HXX[x, pl.ds(z * 4 + c * 2, 2), :]
        HR[ci] = HC[ci]
        c_copy().start()

    def heat_end():
        c_copy().wait_recv()
        for c in range(2):
            for z in range(4):
                for x in range(4):
                    heat_out[pl.ds(z * 16 + x * 4 + c * 2, 2), :] = HR[c, pl.ds(z * 8 + x * 2, 2), :]

    def add(ref, off, wide):
        n = wide // 2
        tail = ref[pl.ds(256, 16), :].astype(F32)
        for i in range(2):
            flat = pl.ds(pl.multiple_of(off + i * n, LANES), n)
            here = pl.ds(pl.multiple_of(off + i * n + LANES, LANES), n)
            extra = []
            for v in range(VARS - 1):
                tend = ref[pl.ds(i * 128 + v * 16, 16), :].astype(F32)
                extra.append(tend[SHARE:])
                total = T1[v, :, here] + PHYS_DT * tend
                out[v, :, flat] = total[:SHARE]
            tend = jnp.concatenate(extra + [tail[i * 8 : i * 8 + 7]], axis=0)
            out[VARS - 1, :, flat] = T1[VARS - 1, :, here][:SHARE] + PHYS_DT * tend

    def finish(c):
        add(TN.at[2, c], col0(g, c), WIDE)
        out_copies(c)[2].wait_recv()
        add(RN.at[0, c], col0(gm, c), WIDE)
        out_copies(c)[3].wait_recv()
        add(RN.at[1, c], col0(gp, c), WIDE)
        for i in range(2):
            out_forwards(c)[i].wait_recv()
            add(RF.at[i, c], pl.multiple_of(col0(go, c) + i * HALF, LANES), HALF)

    edges(S, 0, False)
    start_p1(0)
    forward_in(0)
    send_in(2)
    halve()
    start_p2(0)
    prepare()
    forward_in(1)
    start_p3(0)
    send_in(3)
    substep(S, T1, 0)
    substep(S, T1, 1)
    physics(0)
    substep(S, T1, 2)
    substep(S, T1, 3)
    finish_halo(0)
    edges(T1, 1, True)
    start_p1(1)
    forward_in(2)
    substep(T1, S, 0)
    substep(T1, S, 1)
    start_p2(1)
    physics(1)
    start_p3(1)
    forward_in(3)
    forward_out(0)
    substep(T1, S, 2)
    substep(T1, S, 3)
    finish_halo(1)
    edges(S, 2, True)
    start_p1(2)
    physics(2)
    start_p2(2)
    physics(3)
    start_p3(2)
    forward_out(1)
    heat_z()
    substep(S, T1, 0)
    substep(S, T1, 1)
    forward_out(2)
    heat_x()
    substep(S, T1, 2)
    substep(S, T1, 3)
    heat_c()
    forward_out(3)
    finish_halo(2)
    edges(T1, None, True)
    for c in range(CHUNKS):
        finish(c)
    heat_end()
    for c in range(CHUNKS):
        for copy in in_copies(c) + in_forwards(c) + out_copies(c) + out_forwards(c):
            copy.wait_send()
    for r in range(ROUNDS):
        for k in range(2):
            for copy in p1_copies(r, k):
                copy.wait_send()
            p2_copy(r, k).wait_send()
            for d in (1, 2, 3):
                p3_copy(r, k, d).wait_send()
    for d in (1, 2, 3):
        z_copy(d).wait_send()
        x_copy(d).wait_send()
    c_copy().wait_send()


def write_out(new, heat, new_hbm, heat_hbm, sems):
    copies = [pltpu.make_async_copy(new.at[v], new_hbm.at[v], sems.at[v]) for v in range(VARS)]
    copies.append(pltpu.make_async_copy(heat, heat_hbm, sems.at[VARS]))
    for copy in copies:
        copy.start()
    for copy in copies:
        copy.wait()


def on_device(
    state, courant_x, courant_y, surface, w_in, b_hidden, w_mid, w_out, owner_map, neighbours
):
    smem = pl.BlockSpec(memory_space=pltpu.SMEM)
    vmem = pl.BlockSpec(memory_space=pltpu.VMEM)
    hbm = pl.BlockSpec(memory_space=pltpu.HBM)
    anyw = pl.BlockSpec(memory_space=pl.ANY)
    dma = pltpu.SemaphoreType.DMA
    padded = pltpu.VMEM((VARS, 16, COLS + 2 * LANES), F32)
    halo_shapes = []
    for lead in ((2, 4, 3), (4, 3), (4, 3)) * ROUNDS:
        for rows in GROUP_ROWS:
            halo_shapes.append(pltpu.VMEM(lead + (rows, LANES), BF16))
    new, heat = pl.pallas_call(
        kernel,
        name="couple",
        out_shape=(
            pltpu.VMEM((VARS, SHARE, COLS), F32),
            pltpu.VMEM((64, LANES), F32),
        ),
        in_specs=[smem, smem] + [hbm] * 8,
        out_specs=(vmem, vmem),
        scratch_shapes=[
            pltpu.VMEM((VARS, SHARE, COLS), F32), padded, padded,
            pltpu.VMEM((SHARE, COLS), F32), pltpu.VMEM((SHARE, COLS), F32),
            pltpu.VMEM((16, COLS), F32), pltpu.VMEM((16, COLS), F32),
            pltpu.VMEM((16, COLS), F32), pltpu.VMEM((VARS, 2, 16, LANES), BF16),
            pltpu.VMEM((SSHARE, COLS), BF16),
            pltpu.VMEM((FEAT, HID), BF16),
            pltpu.VMEM((MIDS + 1, HID), F32),
            pltpu.VMEM((MIDS, HID, HID), BF16),
            pltpu.VMEM((OUTF, HID), BF16),
            pltpu.VMEM((4, ROWS, QUARTER), BF16),
            pltpu.VMEM((4 * ROWS, QUARTER), BF16),
            pltpu.VMEM((CHUNKS, ROWS, HALF), BF16), pltpu.VMEM((CHUNKS, ROWS, HALF), BF16),
            pltpu.VMEM((3, CHUNKS, 2 * OROWS, WIDE // 2), BF16),
            pltpu.VMEM((CHUNKS, 2, 2 * OROWS, HALF // 2), BF16),
            pltpu.VMEM((2, CHUNKS, 2 * OROWS, WIDE // 2), BF16),
            pltpu.VMEM((2, CHUNKS, 2 * OROWS, HALF // 2), BF16),
            pltpu.VMEM((CHUNKS, 2 * OROWS, HALF // 2), BF16),
            pltpu.VMEM((CHUNKS, 2 * OROWS, HALF // 2), BF16),
            pltpu.VMEM((HID, 4 * ROWS), BF16),
            pltpu.VMEM((MIDS, HID, HID), BF16),
            pltpu.VMEM((4, OROWS, HID), BF16),
            pltpu.VMEM((MIDS + 1, HID, LANES), F32),
            pltpu.VMEM((VARS, 16, LANES), BF16),
            pltpu.VMEM((VARS, 16, LANES), BF16),
            pltpu.VMEM((16, LANES), F32),
            pltpu.VMEM((64, LANES), F32),
            pltpu.VMEM((4, 16, LANES), F32),
            pltpu.VMEM((4, 16, LANES), F32),
            pltpu.VMEM((4, 16, LANES), F32),
            pltpu.VMEM((2, 32, LANES), F32),
            pltpu.VMEM((2, 32, LANES), F32),
            *halo_shapes,
            dma((CHUNKS, 4)), dma((2,)), dma((5,)),
            dma((CHUNKS, 4)), dma((CHUNKS, 4)), dma((CHUNKS, 2)), dma((CHUNKS, 2)),
            dma((CHUNKS, 4)), dma((CHUNKS, 4)), dma((CHUNKS, 2)), dma((CHUNKS, 2)),
            dma((ROUNDS, 2, 3)), dma((ROUNDS, 2, 3)), dma((ROUNDS, 2)), dma((ROUNDS, 2)),
            dma((ROUNDS, 2, 3)), dma((ROUNDS, 2, 3)),
            dma((3,)), dma((3,)), dma((3,)), dma((3,)), dma((1,)), dma((1,)),
        ],
        compiler_params=pltpu.CompilerParams(
            collective_id=0, has_side_effects=True, vmem_limit_bytes=58 * 2**20
        ),
    )(
        owner_map.reshape(-1), neighbours.T, state, courant_x, courant_y, surface,
        w_in, b_hidden, w_mid, w_out.T,
    )
    return pl.pallas_call(
        write_out,
        name="write_out",
        out_shape=(
            jax.ShapeDtypeStruct((VARS, SHARE, COLS), F32),
            jax.ShapeDtypeStruct((64, LANES), F32),
        ),
        in_specs=[anyw, anyw],
        out_specs=(hbm, hbm),
        scratch_shapes=[dma((VARS + 1,))],
        compiler_params=pltpu.CompilerParams(vmem_limit_bytes=2**20),
    )(
        pltpu.with_memory_space_constraint(new, pltpu.VMEM),
        pltpu.with_memory_space_constraint(heat, pltpu.VMEM),
    )


def solution(mesh):
    placed = (
        P(None, "grp", "patch"), P("grp", "patch"), P("grp", "patch"), P("grp", "patch"),
        P(), P(), P(), P(), P(), P(),
    )
    return jax.shard_map(
        on_device,
        mesh=mesh,
        in_specs=placed,
        out_specs=(P(None, "grp", "patch"), P("grp", "patch")),
        check_vma=False,
    )
```

```python
import jax
import jax.numpy as jnp
from jax import lax
from jax.experimental import pallas as pl
from jax.experimental.pallas import tpu as pltpu
from jax.sharding import PartitionSpec as P

MESH = pl.DeviceIdType.MESH
F32 = jnp.float32
BF16 = jnp.bfloat16

VARS = 9
LEV = 60
SHARE = 15
SURF = 16
SSHARE = 4
HID = 256
MIDS = 3
PX = 64
LANES = 128
COLS = PX * LANES
QUARTER = COLS // 4
ROWS = VARS * 16
OROWS = 136
FEAT = 556
OUTF = 540
CHUNKS = 4
WIDE = QUARTER // CHUNKS
HALF = WIDE // 2
ROUNDS = 3
SPLIT = 5
GROUP_VARS = ((0, SPLIT), (SPLIT, VARS))
GROUP_ROWS = (SPLIT * 16, (VARS - SPLIT) * 16)

KAPPA = 0.24
PHYS_DT = 0.05
HEAT_WEIGHT = 0.125


def kernel(
    owner_ref, nbr_ref, state, courx, coury, surf_in, w_in_in, b_hid_in, w_mid_in, w_out_in,
    out, heat_out,
    ST, S, T1, CX, CY, HX, HY, CK, NS, surf, w_in, b_hid, w_mid, w_out,
    F, X, FP, FM, TN, TF, RN, RF, OP, OM,
    W1, WM, W2, BB, CB, EX, HT, PK, HZ, HZ2, HXX, HC, HR,
    GA0, GB0, SA0, SB0, RA0, RB0, GA1, GB1, SA1, SB1, RA1, RB1, GA2, GB2, SA2, SB2, RA2, RB2,
    load_sem, cour_sem, par_sem,
    in_s, in_r, fw_s, fw_r, out_s, out_r, of_s, of_r,
    p1_s, p1_r, p2_s, p2_r, p3_s, p3_r, hz_s, hz_r, hx_s, hx_r, hc_s, hc_r,
):
    g = lax.axis_index("grp")
    p = lax.axis_index("patch")
    zi, xi, ci = p // 8, (p // 2) % 4, p % 2
    gp, gm, go = (g + 1) % 4, (g + 3) % 4, (g + 2) % 4

    def rcopy(src, dst, ss, rs, dev):
        return pltpu.make_async_remote_copy(
            src_ref=src, dst_ref=dst, send_sem=ss, recv_sem=rs, device_id=dev, device_id_type=MESH
        )

    def col0(q, c):
        return pl.multiple_of(q * QUARTER + c * WIDE, LANES)

    order = (go, gp, gm, g)

    def load(c, i):
        off = col0(order[i], c)
        return pltpu.make_async_copy(
            state.at[:, :, pl.ds(off, WIDE)],
            ST.at[:, :, pl.ds(off, WIDE)],
            load_sem.at[c, i],
        )

    params = tuple(
        pltpu.make_async_copy(src, dst, par_sem.at[i])
        for i, (src, dst) in enumerate(
            ((surf_in, surf), (w_in_in, w_in), (b_hid_in, b_hid), (w_mid_in, w_mid), (w_out_in, w_out))
        )
    )
    cour = (
        pltpu.make_async_copy(courx, CX, cour_sem.at[0]),
        pltpu.make_async_copy(coury, CY, cour_sem.at[1]),
    )

    barrier = pltpu.get_barrier_semaphore()
    for other in (gp, gm, go):
        pl.semaphore_signal(barrier, inc=1, device_id=(other, p), device_id_type=MESH)
    for d in (1, 2, 3):
        pl.semaphore_signal(
            barrier, inc=1, device_id=(g, zi * 8 + ((xi + d) % 4) * 2 + ci), device_id_type=MESH
        )
        pl.semaphore_signal(
            barrier, inc=1, device_id=(g, ((zi + d) % 4) * 8 + xi * 2 + ci), device_id_type=MESH
        )
    pl.semaphore_signal(barrier, inc=1, device_id=(g, p + 1 - 2 * ci), device_id_type=MESH)

    params[0].start()
    for c in range(CHUNKS):
        for i in range(4):
            load(c, i).start()
    for copy in params[1:] + cour:
        copy.start()
    params[0].wait()

    def cast(q, c, own):
        off = col0(q, c)
        here = pl.multiple_of(off + LANES, LANES)
        for v in range(VARS):
            value = ST[v, :, pl.ds(off, WIDE)]
            if v < SSHARE:
                extra = surf[v : v + 1, pl.ds(off, WIDE)].astype(F32)
            else:
                extra = jnp.zeros((1, WIDE), F32)
            value = jnp.concatenate([value, extra], axis=0)
            S[v, :, pl.ds(here, WIDE)] = value
            value = value.astype(BF16)
            if not own:
                F[q, pl.ds(v * 16, 16), pl.ds(c * WIDE, WIDE)] = value
            else:
                X[pl.ds(pl.multiple_of(g * ROWS + v * 16, 16), 16), pl.ds(c * WIDE, WIDE)] = value

    mine = pl.ds(pl.multiple_of(g * ROWS, 16), ROWS)
    prev_rows = pl.ds(pl.multiple_of(gm * ROWS, 16), ROWS)
    next_rows = pl.ds(pl.multiple_of(gp * ROWS, 16), ROWS)

    def in_copies(c):
        lo, hi, whole = pl.ds(c * WIDE, HALF), pl.ds(c * WIDE + HALF, HALF), pl.ds(c * WIDE, WIDE)
        return (
            rcopy(F.at[go, :, lo], FP.at[c], in_s.at[c, 0], in_r.at[c, 0], (gp, p)),
            rcopy(F.at[go, :, hi], FM.at[c], in_s.at[c, 1], in_r.at[c, 1], (gm, p)),
            rcopy(F.at[gp, :, whole], X.at[mine, whole], in_s.at[c, 2], in_r.at[c, 2], (gp, p)),
            rcopy(F.at[gm, :, whole], X.at[mine, whole], in_s.at[c, 3], in_r.at[c, 3], (gm, p)),
        )

    def in_forwards(c):
        lo, hi = pl.ds(c * WIDE, HALF), pl.ds(c * WIDE + HALF, HALF)
        return (
            rcopy(FP.at[c], X.at[prev_rows, lo], fw_s.at[c, 0], fw_r.at[c, 0], (gp, p)),
            rcopy(FM.at[c], X.at[next_rows, hi], fw_s.at[c, 1], fw_r.at[c, 1], (gm, p)),
        )

    def out_copies(c):
        return (
            rcopy(TF.at[c, 0], OP.at[c], out_s.at[c, 0], out_r.at[c, 0], (gp, p)),
            rcopy(TF.at[c, 1], OM.at[c], out_s.at[c, 1], out_r.at[c, 1], (gm, p)),
            rcopy(TN.at[0, c], RN.at[0, c], out_s.at[c, 2], out_r.at[c, 2], (gp, p)),
            rcopy(TN.at[1, c], RN.at[1, c], out_s.at[c, 3], out_r.at[c, 3], (gm, p)),
        )

    def out_forwards(c):
        return (
            rcopy(OP.at[c], RF.at[0, c], of_s.at[c, 0], of_r.at[c, 0], (gp, p)),
            rcopy(OM.at[c], RF.at[1, c], of_s.at[c, 1], of_r.at[c, 1], (gm, p)),
        )

    def send_in(c):
        for copy in in_copies(c):
            copy.start()

    for c in range(CHUNKS):
        for i in range(3):
            load(c, i).wait()
            cast(order[i], c, False)
        if c == 0:
            pl.semaphore_wait(barrier, 10)
        if c < 2:
            send_in(c)
    for c in range(CHUNKS):
        load(c, 3).wait()
        cast(g, c, True)

    halo = (
        ((GA0, SA0, RA0), (GB0, SB0, RB0)),
        ((GA1, SA1, RA1), (GB1, SB1, RB1)),
        ((GA2, SA2, RA2), (GB2, SB2, RB2)),
    )
    first = (xi, zi)
    second = (zi, xi)
    even = lax.broadcasted_iota(jnp.int32, (16, LANES), 1) % 2 == 0

    def patch_of(k, one, two, core):
        return two * 8 + one * 2 + core if k == 0 else one * 8 + two * 2 + core

    def spots(k, n):
        z, x, core = n // 8, (n // 2) % 4, n % 2
        return (x, z, core) if k == 0 else (z, x, core)

    def p1_copies(r, k):
        G = halo[r][k][0]
        return [
            rcopy(
                G.at[ci, first[k]], G.at[ci, first[k]], p1_s.at[r, k, d - 1], p1_r.at[r, k, d - 1],
                (g, patch_of(k, (first[k] + d) % 4, second[k], ci)),
            )
            for d in (2, 1, 3)
        ]

    def p2_copy(r, k):
        G = halo[r][k][0]
        return rcopy(
            G.at[ci], G.at[ci], p2_s.at[r, k], p2_r.at[r, k],
            (g, patch_of(k, first[k], second[k], 1 - ci)),
        )

    def p3_copy(r, k, d):
        _, Sd, R = halo[r][k]
        return rcopy(
            Sd.at[d], R.at[second[k]], p3_s.at[r, k, d - 1], p3_r.at[r, k, d - 1],
            (g, patch_of(k, first[k], (second[k] + d) % 4, ci)),
        )

    def put_edge(r, strip, v, value):
        k = 0 if v < SPLIT else 1
        G = halo[r][k][0]
        G[ci, first[k], strip, pl.ds((v - GROUP_VARS[k][0]) * 16, 16), :] = value

    def start_p1(r):
        for k in range(2):
            for copy in p1_copies(r, k):
                copy.start()

    def start_p2(r):
        for k in range(2):
            for copy in p1_copies(r, k):
                copy.wait_recv()
            p2_copy(r, k).start()

    def start_p3(r):
        for k in range(2):
            G, Sd, R = halo[r][k]
            p2_copy(r, k).wait_recv()
            for d in (2, 1, 3, 0):
                t = patch_of(k, first[k], (second[k] + d) % 4, ci)
                at = [spots(k, nbr_ref[j, t]) for j in range(4)]
                north = G[at[0][2], at[0][0], 1]
                south = G[at[1][2], at[1][0], 0]
                if d == 0:
                    R[second[k], 0] = north
                    R[second[k], 1] = south
                else:
                    Sd[d, 0] = north
                    Sd[d, 1] = south
                for v in range(GROUP_ROWS[k] // 16):
                    rows = pl.ds(v * 16, 16)
                    west = G[at[2][2], at[2][0], 2, rows].astype(F32)
                    east = G[at[3][2], at[3][0], 2, rows].astype(F32)
                    mixed = jnp.where(even, east, west).astype(BF16)
                    if d == 0:
                        R[second[k], 2, rows] = mixed
                    else:
                        Sd[d, 2, rows] = mixed
                if d:
                    p3_copy(r, k, d).start()

    def finish_halo(r):
        for k in range(2):
            R = halo[r][k][2]
            for d in (2, 1, 3):
                p3_copy(r, k, d).wait_recv()
            at = [spots(k, nbr_ref[j, p])[1] for j in range(4)]
            for v in range(*GROUP_VARS[k]):
                rows = pl.ds((v - GROUP_VARS[k][0]) * 16, 16)
                NS[v, 0] = R[at[0], 0, rows]
                NS[v, 1] = R[at[1], 1, rows]
                west = pltpu.roll(R[at[2], 2, rows].astype(F32), 1, 1)
                east = pltpu.roll(R[at[3], 2, rows].astype(F32), LANES - 1, 1)
                CB[v] = jnp.where(even, west, east).astype(BF16)

    lane = lax.broadcasted_iota(jnp.int32, (16, LANES), 1)

    def edges(T, r, beside):
        def pick(v, carry):
            acc = jnp.zeros((16, LANES), BF16)
            for x in range(PX):
                here = pl.ds((x + 1) * LANES, LANES)
                tile = T[v, :, here]
                if beside:
                    flat = pl.ds(x * LANES, LANES)
                    side = pltpu.roll(CB[v], (LANES - 2 * x) % LANES, 1).astype(F32)
                    tile = tile + CK[:, flat] * side
                    if x == 0:
                        tile = tile + (KAPPA + HX[:, flat]) * NS[v, 0].astype(F32)
                    if x == PX - 1:
                        tile = tile + (KAPPA - HX[:, flat]) * NS[v, 1].astype(F32)
                    T[v, :, here] = tile
                if r is not None:
                    mask = (lane == 2 * x) | (lane == (2 * x + LANES - 1) % LANES)
                    acc = jnp.where(mask, pltpu.roll(tile.astype(BF16), 2 * x, 1), acc)
            EX[v] = acc
            return carry

        lax.fori_loop(0, VARS, pick, 0)
        if r is None:
            return
        for v in range(VARS):
            put_edge(r, 0, v, T[v, :, pl.ds(LANES, LANES)].astype(BF16))
            put_edge(r, 1, v, T[v, :, pl.ds(COLS, LANES)].astype(BF16))
            put_edge(r, 2, v, EX[v])

    def substep(T, N, part):
        def step(x, carry):
            here = pl.ds(pl.multiple_of((x + 1) * LANES, LANES), LANES)
            above = pl.ds(pl.multiple_of(x * LANES, LANES), LANES)
            below = pl.ds(pl.multiple_of((x + 2) * LANES, LANES), LANES)
            flat = pl.ds(pl.multiple_of(x * LANES, LANES), LANES)
            hx = HX[:, flat]
            hy = HY[:, flat]
            cn, cs = KAPPA + hx, KAPPA - hx
            cw = jnp.where(lane == 0, 0.0, KAPPA + hy)
            ce = jnp.where(lane == LANES - 1, 0.0, KAPPA - hy)
            for v in range(VARS):
                c = T[v, :, here]
                N[v, :, here] = (
                    (1.0 - 4.0 * KAPPA) * c
                    + (cn * T[v, :, above] + cs * T[v, :, below])
                    + (cw * pltpu.roll(c, 1, 1) + ce * pltpu.roll(c, LANES - 1, 1))
                )
            return carry

        lax.fori_loop(part * 16, part * 16 + 16, step, 0, unroll=8)

    def halve():
        for copy in cour:
            copy.wait()
        blank = jnp.zeros((1, COLS), F32)
        HX[...] = jnp.concatenate([0.5 * CX[...], blank], axis=0)
        half = jnp.concatenate([0.5 * CY[...], blank], axis=0)
        HY[...] = half
        place = lax.broadcasted_iota(jnp.int32, (16, COLS), 1) & (LANES - 1)
        CK[...] = jnp.where(
            place == 0, KAPPA + half, jnp.where(place == LANES - 1, KAPPA - half, 0.0)
        )
        for T in (S, T1):
            T[:, :, pl.ds(0, LANES)] = jnp.zeros((VARS, 16, LANES), F32)
            T[:, :, pl.ds(LANES + COLS, LANES)] = jnp.zeros((VARS, 16, LANES), F32)

    def prepare():
        for copy in params[1:]:
            copy.wait()
        j = lax.broadcasted_iota(jnp.int32, (4 * ROWS, 1), 0)
        grp = (j >= ROWS).astype(jnp.int32) + (j >= 2 * ROWS).astype(jnp.int32) + (j >= 3 * ROWS).astype(jnp.int32)
        rest = j - grp * ROWS
        var, lev = rest >> 4, rest & 15
        state_row = var * LEV + grp * SHARE + lev
        surf_row = jnp.where(var < SSHARE, VARS * LEV + grp * SSHARE + var, -1)
        source = jnp.where(lev < SHARE, state_row, surf_row)
        pick = (source == lax.broadcasted_iota(jnp.int32, (4 * ROWS, FEAT), 1)).astype(F32).astype(BF16)
        placed = jnp.dot(pick, w_in[...], preferred_element_type=F32)
        W1[...] = placed.T.astype(BF16)
        j = lax.broadcasted_iota(jnp.int32, (4 * OROWS, 1), 0)
        grp = (j >= OROWS).astype(jnp.int32) + (j >= 2 * OROWS).astype(jnp.int32) + (j >= 3 * OROWS).astype(jnp.int32)
        rest = j - grp * OROWS
        var, lev = rest >> 4, rest & 15
        last = (VARS - 1) * LEV + grp * SHARE
        main_row = jnp.where(lev < SHARE, var * LEV + grp * SHARE + lev, last + var)
        tail_row = jnp.where(rest < OROWS - 1, last + rest - 120, -1)
        source = jnp.where(rest < 128, main_row, tail_row)
        pick = (source == lax.broadcasted_iota(jnp.int32, (4 * OROWS, OUTF), 1)).astype(F32).astype(BF16)
        placed = jnp.dot(pick, w_out[...], preferred_element_type=F32)
        for d in range(4):
            W2[d] = placed[d * OROWS : (d + 1) * OROWS].astype(BF16)
        for i in range(MIDS):
            WM[i] = w_mid[i].astype(F32).T.astype(BF16)
        for i in range(MIDS + 1):
            BB[i] = jnp.broadcast_to(b_hid[i : i + 1, :], (LANES, HID)).T

    def silu(i, pre):
        half = 0.5 * (pre + jnp.concatenate([BB[i]] * (WIDE // LANES), axis=1))
        return (half + half * jnp.tanh(half)).astype(BF16)

    def physics(c):
        whole = pl.ds(c * WIDE, WIDE)
        in_copies(c)[2].wait_recv()
        in_copies(c)[3].wait_recv()
        for copy in in_forwards(c):
            copy.wait_recv()
        hidden = silu(0, jnp.dot(W1[...], X[:, whole], preferred_element_type=F32))
        for i in range(MIDS):
            hidden = silu(i + 1, jnp.dot(WM[i], hidden, preferred_element_type=F32))
        total = jnp.zeros((1, WIDE), F32)
        level = lax.broadcasted_iota(jnp.int32, (16, WIDE), 0)
        def pack(ref, tend):
            n = tend.shape[1] // 2
            ref[pl.ds(0, 128), :] = tend[:128, :n].astype(BF16)
            ref[pl.ds(128, 128), :] = tend[:128, n:].astype(BF16)
            ref[pl.ds(256, 16), :] = jnp.concatenate([tend[128:, :n], tend[128:, n:]], axis=0).astype(BF16)

        for i, d in enumerate((gp, gm, g, go)):
            tend = jnp.dot(W2[d], hidden, preferred_element_type=F32)
            if i < 3:
                pack(TN.at[i, c], tend)
            else:
                pack(TF.at[c, 0], tend[:, :HALF])
                pack(TF.at[c, 1], tend[:, HALF:])
            first_var = jnp.where(level < SHARE, tend[:16].astype(BF16).astype(F32), 0.0)
            total = total + jnp.sum(first_var, axis=0, keepdims=True)
        total = HEAT_WEIGHT * total
        for i in range(WIDE // LANES):
            HT[pl.ds(c * (WIDE // LANES) + i, 1), :] = total[:, i * LANES : (i + 1) * LANES]
        for copy in out_copies(c):
            copy.start()

    def forward_in(c):
        copies = in_copies(c)
        forwards = in_forwards(c)
        for i in range(2):
            copies[i].wait_recv()
            forwards[i].start()

    def forward_out(c):
        copies = out_copies(c)
        forwards = out_forwards(c)
        for i in range(2):
            copies[i].wait_recv()
            forwards[i].start()

    def z_copy(d):
        z = (zi + d) % 4
        return rcopy(
            PK.at[pl.ds(pl.multiple_of(z * 16, 16), 16)], HZ.at[zi], hz_s.at[d - 1], hz_r.at[d - 1],
            (g, z * 8 + xi * 2 + ci),
        )

    def x_copy(d):
        x = (xi + d) % 4
        return rcopy(
            HZ2.at[x], HXX.at[xi], hx_s.at[d - 1], hx_r.at[d - 1], (g, zi * 8 + x * 2 + ci)
        )

    def c_copy():
        return rcopy(
            HC.at[1 - ci], HR.at[ci], hc_s.at[0], hc_r.at[0], (g, p + 1 - 2 * ci)
        )

    def heat_z():
        owner = [owner_ref[p * PX + g * 16 + b] for b in range(16)]
        slot = []
        for b in range(16):
            rank = jnp.int32(0)
            for before in range(b):
                rank = rank + (owner[before] == owner[b]).astype(jnp.int32)
            slot.append(owner[b] * 2 + rank)
        rows = lax.broadcasted_iota(jnp.int32, (64, LANES), 0)
        table = jnp.zeros((64, LANES), F32)
        for b in range(16):
            table = jnp.where(rows == slot[b], jnp.broadcast_to(HT[pl.ds(b, 1), :], (64, LANES)), table)
        PK[...] = table
        HZ[zi] = PK[pl.ds(pl.multiple_of(zi * 16, 16), 16), :]
        for d in (2, 1, 3):
            z_copy(d).start()

    def heat_x():
        for d in (2, 1, 3):
            z_copy(d).wait_recv()
        for z in range(4):
            for x in range(4):
                HZ2[x, pl.ds(z * 4, 4), :] = HZ[z, pl.ds(x * 4, 4), :]
        HXX[xi] = HZ2[xi]
        for d in (2, 1, 3):
            x_copy(d).start()

    def heat_c():
        for d in (2, 1, 3):
            x_copy(d).wait_recv()
        for c in range(2):
            for z in range(4):
                for x in range(4):
                    HC[c, pl.ds(z * 8 + x * 2, 2), :] = HXX[x, pl.ds(z * 4 + c * 2, 2), :]
        HR[ci] = HC[ci]
        c_copy().start()

    def heat_end():
        c_copy().wait_recv()
        for c in range(2):
            for z in range(4):
                for x in range(4):
                    heat_out[pl.ds(z * 16 + x * 4 + c * 2, 2), :] = HR[c, pl.ds(z * 8 + x * 2, 2), :]

    def add(ref, off, wide):
        n = wide // 2
        tail = ref[pl.ds(256, 16), :].astype(F32)
        for i in range(2):
            flat = pl.ds(pl.multiple_of(off + i * n, LANES), n)
            here = pl.ds(pl.multiple_of(off + i * n + LANES, LANES), n)
            extra = []
            for v in range(VARS - 1):
                tend = ref[pl.ds(i * 128 + v * 16, 16), :].astype(F32)
                extra.append(tend[SHARE:])
                total = T1[v, :, here] + PHYS_DT * tend
                out[v, :, flat] = total[:SHARE]
            tend = jnp.concatenate(extra + [tail[i * 8 : i * 8 + 7]], axis=0)
            out[VARS - 1, :, flat] = T1[VARS - 1, :, here][:SHARE] + PHYS_DT * tend

    def finish(c):
        add(TN.at[2, c], col0(g, c), WIDE)
        out_copies(c)[2].wait_recv()
        add(RN.at[0, c], col0(gm, c), WIDE)
        out_copies(c)[3].wait_recv()
        add(RN.at[1, c], col0(gp, c), WIDE)
        for i in range(2):
            out_forwards(c)[i].wait_recv()
            add(RF.at[i, c], pl.multiple_of(col0(go, c) + i * HALF, LANES), HALF)

    edges(S, 0, False)
    start_p1(0)
    forward_in(0)
    send_in(2)
    halve()
    start_p2(0)
    prepare()
    forward_in(1)
    start_p3(0)
    send_in(3)
    substep(S, T1, 0)
    substep(S, T1, 1)
    substep(S, T1, 2)
    substep(S, T1, 3)
    finish_halo(0)
    edges(T1, 1, True)
    start_p1(1)
    physics(0)
    forward_in(2)
    substep(T1, S, 0)
    substep(T1, S, 1)
    start_p2(1)
    physics(1)
    start_p3(1)
    forward_in(3)
    forward_out(0)
    substep(T1, S, 2)
    substep(T1, S, 3)
    finish_halo(1)
    edges(S, 2, True)
    start_p1(2)
    physics(2)
    start_p2(2)
    physics(3)
    start_p3(2)
    forward_out(1)
    heat_z()
    substep(S, T1, 0)
    substep(S, T1, 1)
    forward_out(2)
    heat_x()
    substep(S, T1, 2)
    substep(S, T1, 3)
    heat_c()
    forward_out(3)
    finish_halo(2)
    edges(T1, None, True)
    for c in range(CHUNKS):
        finish(c)
    heat_end()
    for c in range(CHUNKS):
        for copy in in_copies(c) + in_forwards(c) + out_copies(c) + out_forwards(c):
            copy.wait_send()
    for r in range(ROUNDS):
        for k in range(2):
            for copy in p1_copies(r, k):
                copy.wait_send()
            p2_copy(r, k).wait_send()
            for d in (1, 2, 3):
                p3_copy(r, k, d).wait_send()
    for d in (1, 2, 3):
        z_copy(d).wait_send()
        x_copy(d).wait_send()
    c_copy().wait_send()


def write_out(new, heat, new_hbm, heat_hbm, sems):
    copies = [pltpu.make_async_copy(new.at[v], new_hbm.at[v], sems.at[v]) for v in range(VARS)]
    copies.append(pltpu.make_async_copy(heat, heat_hbm, sems.at[VARS]))
    for copy in copies:
        copy.start()
    for copy in copies:
        copy.wait()


def on_device(
    state, courant_x, courant_y, surface, w_in, b_hidden, w_mid, w_out, owner_map, neighbours
):
    smem = pl.BlockSpec(memory_space=pltpu.SMEM)
    vmem = pl.BlockSpec(memory_space=pltpu.VMEM)
    hbm = pl.BlockSpec(memory_space=pltpu.HBM)
    anyw = pl.BlockSpec(memory_space=pl.ANY)
    dma = pltpu.SemaphoreType.DMA
    padded = pltpu.VMEM((VARS, 16, COLS + 2 * LANES), F32)
    halo_shapes = []
    for lead in ((2, 4, 3), (4, 3), (4, 3)) * ROUNDS:
        for rows in GROUP_ROWS:
            halo_shapes.append(pltpu.VMEM(lead + (rows, LANES), BF16))
    new, heat = pl.pallas_call(
        kernel,
        name="couple",
        out_shape=(
            pltpu.VMEM((VARS, SHARE, COLS), F32),
            pltpu.VMEM((64, LANES), F32),
        ),
        in_specs=[smem, smem] + [hbm] * 8,
        out_specs=(vmem, vmem),
        scratch_shapes=[
            pltpu.VMEM((VARS, SHARE, COLS), F32), padded, padded,
            pltpu.VMEM((SHARE, COLS), F32), pltpu.VMEM((SHARE, COLS), F32),
            pltpu.VMEM((16, COLS), F32), pltpu.VMEM((16, COLS), F32),
            pltpu.VMEM((16, COLS), F32), pltpu.VMEM((VARS, 2, 16, LANES), BF16),
            pltpu.VMEM((SSHARE, COLS), BF16),
            pltpu.VMEM((FEAT, HID), BF16),
            pltpu.VMEM((MIDS + 1, HID), F32),
            pltpu.VMEM((MIDS, HID, HID), BF16),
            pltpu.VMEM((OUTF, HID), BF16),
            pltpu.VMEM((4, ROWS, QUARTER), BF16),
            pltpu.VMEM((4 * ROWS, QUARTER), BF16),
            pltpu.VMEM((CHUNKS, ROWS, HALF), BF16), pltpu.VMEM((CHUNKS, ROWS, HALF), BF16),
            pltpu.VMEM((3, CHUNKS, 2 * OROWS, WIDE // 2), BF16),
            pltpu.VMEM((CHUNKS, 2, 2 * OROWS, HALF // 2), BF16),
            pltpu.VMEM((2, CHUNKS, 2 * OROWS, WIDE // 2), BF16),
            pltpu.VMEM((2, CHUNKS, 2 * OROWS, HALF // 2), BF16),
            pltpu.VMEM((CHUNKS, 2 * OROWS, HALF // 2), BF16),
            pltpu.VMEM((CHUNKS, 2 * OROWS, HALF // 2), BF16),
            pltpu.VMEM((HID, 4 * ROWS), BF16),
            pltpu.VMEM((MIDS, HID, HID), BF16),
            pltpu.VMEM((4, OROWS, HID), BF16),
            pltpu.VMEM((MIDS + 1, HID, LANES), F32),
            pltpu.VMEM((VARS, 16, LANES), BF16),
            pltpu.VMEM((VARS, 16, LANES), BF16),
            pltpu.VMEM((16, LANES), F32),
            pltpu.VMEM((64, LANES), F32),
            pltpu.VMEM((4, 16, LANES), F32),
            pltpu.VMEM((4, 16, LANES), F32),
            pltpu.VMEM((4, 16, LANES), F32),
            pltpu.VMEM((2, 32, LANES), F32),
            pltpu.VMEM((2, 32, LANES), F32),
            *halo_shapes,
            dma((CHUNKS, 4)), dma((2,)), dma((5,)),
            dma((CHUNKS, 4)), dma((CHUNKS, 4)), dma((CHUNKS, 2)), dma((CHUNKS, 2)),
            dma((CHUNKS, 4)), dma((CHUNKS, 4)), dma((CHUNKS, 2)), dma((CHUNKS, 2)),
            dma((ROUNDS, 2, 3)), dma((ROUNDS, 2, 3)), dma((ROUNDS, 2)), dma((ROUNDS, 2)),
            dma((ROUNDS, 2, 3)), dma((ROUNDS, 2, 3)),
            dma((3,)), dma((3,)), dma((3,)), dma((3,)), dma((1,)), dma((1,)),
        ],
        compiler_params=pltpu.CompilerParams(
            collective_id=0, has_side_effects=True, vmem_limit_bytes=58 * 2**20
        ),
    )(
        owner_map.reshape(-1), neighbours.T, state, courant_x, courant_y, surface,
        w_in, b_hidden, w_mid, w_out.T,
    )
    return pl.pallas_call(
        write_out,
        name="write_out",
        out_shape=(
            jax.ShapeDtypeStruct((VARS, SHARE, COLS), F32),
            jax.ShapeDtypeStruct((64, LANES), F32),
        ),
        in_specs=[anyw, anyw],
        out_specs=(hbm, hbm),
        scratch_shapes=[dma((VARS + 1,))],
        compiler_params=pltpu.CompilerParams(vmem_limit_bytes=2**20),
    )(
        pltpu.with_memory_space_constraint(new, pltpu.VMEM),
        pltpu.with_memory_space_constraint(heat, pltpu.VMEM),
    )


def solution(mesh):
    placed = (
        P(None, "grp", "patch"), P("grp", "patch"), P("grp", "patch"), P("grp", "patch"),
        P(), P(), P(), P(), P(), P(),
    )
    return jax.shard_map(
        on_device,
        mesh=mesh,
        in_specs=placed,
        out_specs=(P(None, "grp", "patch"), P("grp", "patch")),
        check_vma=False,
    )
```
